256 devices in a mesh: dp: 4 (over x), ctx: 64 (over y, z, core).
Axes of the slice: x: 4, y: 4, z: 8, core: 2. Of those that a mesh axis runs over, the one named last changes fastest.
Arguments:
- queries: bfloat16 [4, 12288, 8192], P('dp', 'ctx'), may hold values from -6 to 6
- keys: bfloat16 [4, 12288, 8192], P('dp', 'ctx'), may hold values from -6 to 6
- values: bfloat16 [4, 12288, 8192], P('dp', 'ctx'), may hold values from -6 to 6
- log_decay: bfloat16 [4, 12288, 64], P('dp', 'ctx'), may hold values from -1 to 0
- starts: int32 [4, 3], P('dp'), may hold values from 0 to 12032, as said below
- norm_gain: float32 [8192], replicated, may hold values from 0.1 to 1.9
- router_new: bfloat16 [8192, 32], replicated, may hold values from -0.0625 to 0.0625
- router_old: bfloat16 [8192, 32], replicated, may hold values from -0.0625 to 0.0625
Outputs:
- logits_new: float32 [4, 12288, 32], P('dp', 'ctx')
- divergence: float32 [], replicated
The draws below stay inside these ranges and needn't reach their ends.
Inputs may be any that keep to these rules, and one draw needn't show every extreme that they name: `starts`: each row begins with 0 and rises strictly; every entry is a multiple of 256.
All inputs are finite; a program needn't handle non-finite values.
Results may differ from the reference program's by a relative error of at most 0.0037.
Values may be sent and summed in bfloat16 or wider, within the bound.
A program may use at most 128 MiB of HBM per device.

```python
import jax
import jax.numpy as jnp
from jax import lax

HEADS = 64
HD = 128
EXPERTS = 32
TOK_DEV = 192
ALIGN = 256
SEGS = 3
SLAB_TOKENS = 12288
BLOCK = 1536
ROLLOUT_SLABS = 4


def draw_log_decay(key, part):
    key = jax.random.fold_in(key, 11)
    random_key_list = jax.random.split(key, 7)
    fast_share = 0.5
    fast = jax.random.uniform(random_key_list[0], (ROLLOUT_SLABS, 1, HEADS)) < fast_share
    fast_rate = jax.random.uniform(random_key_list[1], (ROLLOUT_SLABS, 1, HEADS), minval=1.0 / 50.0, maxval=1.0 / 30.0)
    slow_rate = jax.random.uniform(random_key_list[2], (ROLLOUT_SLABS, 1, HEADS), minval=0.1, maxval=1.0) * 0.25 / SLAB_TOKENS
    decay_rate = jnp.where(fast, fast_rate, slow_rate)
    low_device = jax.random.uniform(random_key_list[3], (ROLLOUT_SLABS, SLAB_TOKENS // TOK_DEV, 1, 1)) < 0.5
    device_multiplier = jnp.where(low_device, 0.02, 1.98).astype(jnp.float32)
    device_multiplier = jnp.broadcast_to(device_multiplier, (ROLLOUT_SLABS, SLAB_TOKENS // TOK_DEV, TOK_DEV, 1)).reshape(ROLLOUT_SLABS, SLAB_TOKENS, 1)
    coarse_estimate = jax.random.uniform(random_key_list[4], (ROLLOUT_SLABS, SLAB_TOKENS, HEADS), minval=0.5, maxval=1.5)
    spike_position = jax.random.uniform(random_key_list[5], (ROLLOUT_SLABS, SLAB_TOKENS, 1)) < 2.0 / SLAB_TOKENS
    spike_length = jnp.log(jax.random.uniform(random_key_list[6], (ROLLOUT_SLABS, SLAB_TOKENS, 1), minval=0.5, maxval=0.8))
    decay_lambda = -decay_rate * device_multiplier * coarse_estimate + jnp.where(spike_position, spike_length, 0.0)
    return decay_lambda.astype(jnp.float32).astype(jnp.bfloat16)


def draw_starts(key, part):
    key = jax.random.fold_in(key, 23)
    slab_keys = jax.random.split(key, ROLLOUT_SLABS)

    def one_slab(slab_key):
        picked = jax.random.permutation(slab_key, SLAB_TOKENS // ALIGN - 1)[:SEGS - 1] + 1
        ordered = jnp.sort(picked).astype(jnp.int32)
        return jnp.concatenate([jnp.zeros((1,), jnp.int32), ordered])
    table = jax.vmap(one_slab)(slab_keys).astype(jnp.int32)
    table = table.at[0, SEGS - 1].set(jnp.int32(SLAB_TOKENS // ALIGN - 1))
    return (table * ALIGN).astype(jnp.int32)


def shard_levels(rng, shape, shards, low, top_value):
    factor_of = 1.0
    for axis_at, blocks in shards:
        steps = jax.random.uniform(jax.random.fold_in(jax.random.fold_in(rng, 6), axis_at), (blocks,), jnp.float32, low / len(shards), top_value / len(shards))
        factor_of = factor_of * jnp.repeat(jnp.exp(steps), shape[axis_at] // blocks).reshape((-1,) + (1,) * (len(shape) - 1 - axis_at))
    return factor_of


def bell_draw(key, shape, scale, bound, shards=(), kind=jnp.bfloat16):
    level = shard_levels(key, shape, shards, -0.22, 0.18) if shards else 1.0
    values = jax.random.normal(key, shape, jnp.float32) * scale * level
    return jnp.minimum(jnp.maximum(values, -bound), bound).astype(kind)


def setup_inputs(seed: int = 0) -> dict:
    key_list = jax.random.split(jax.random.key(seed), 9)
    return {
        "queries": bell_draw(key_list[0], (ROLLOUT_SLABS, SLAB_TOKENS, HEADS * HD), 1.0, 6.0, ((0, 4), (1, 64))),
        "keys": bell_draw(key_list[1], (ROLLOUT_SLABS, SLAB_TOKENS, HEADS * HD), 1.0, 6.0, ((0, 4), (1, 64))),
        "values": bell_draw(key_list[2], (ROLLOUT_SLABS, SLAB_TOKENS, HEADS * HD), 1.0, 6.0, ((0, 4), (1, 64))),
        "log_decay": draw_log_decay(jax.random.fold_in(key_list[8], 71), 0),
        "starts": draw_starts(jax.random.fold_in(key_list[8], 71), 0),
        "norm_gain": jnp.clip(1.0 + 0.18 * jax.random.normal(key_list[5], (HEADS * HD,), jnp.float32), 0.1, 1.9),
        "router_new": bell_draw(key_list[6], (HEADS * HD, EXPERTS), (HEADS * HD) ** -0.5, 0.0625),
        "router_old": bell_draw(key_list[7], (HEADS * HD, EXPERTS), (HEADS * HD) ** -0.5, 0.0625),
    }


def block_weights(lam_b, seg_b):
    c = jnp.cumsum(lam_b)
    count = lam_b.shape[0]
    later = lax.broadcasted_iota(jnp.int32, (count, count), 0)
    earlier = lax.broadcasted_iota(jnp.int32, (count, count), 1)
    mask = (seg_b[:, None] == seg_b[None, :]) & (later >= earlier)
    weight = jnp.where(mask, jnp.exp(jnp.where(mask, c[:, None] - c[None, :], 0.0)), 0.0)
    return (c, weight)

def block_state(state, last_seg, c, kb, vb, seg_b):
    seg_end = seg_b[-1]
    tail = jnp.exp(c[-1] - c) * (seg_b == seg_end).astype(jnp.float32)
    keep = jnp.where(seg_end == last_seg, jnp.exp(c[-1]), 0.0)
    added = jnp.dot((kb.astype(jnp.float32) * tail[:, None]).T, vb.astype(jnp.float32), precision=lax.Precision.HIGHEST)
    return (keep * state + added, seg_end)

def block_output(state, last_seg, c, weight, qb, kb, vb, seg_b, gain):
    scores = lax.dot_general(qb, kb, (((1,), (1,)), ((), ())), preferred_element_type=jnp.float32)
    probs = (scores * weight).astype(jnp.bfloat16)
    intra = jnp.dot(probs, vb, preferred_element_type=jnp.float32)
    carried = jnp.exp(c) * (seg_b == last_seg).astype(jnp.float32)
    inter = carried[:, None] * jnp.dot(qb.astype(jnp.float32), state, precision=lax.Precision.HIGHEST)
    total = intra + inter
    meansq = lax.optimization_barrier(jnp.mean(total * total, axis=1, keepdims=True)) + 1e-06
    return (total * lax.rsqrt(meansq) * gain).astype(jnp.bfloat16)

def head_attention(qh, kh, vh, decay_lambda, seg, gain, block):
    length, width = qh.shape
    blocks = length // block
    xs = (qh.reshape(blocks, block, width), kh.reshape(blocks, block, width), vh.reshape(blocks, block, width), decay_lambda.reshape(blocks, block), seg.reshape(blocks, block))

    def step(carry, item):
        state, last_seg = carry
        qb, kb, vb, lb, sb = item
        c, weight = block_weights(lb, sb)
        out = block_output(state, last_seg, c, weight, qb, kb, vb, sb, gain)
        return (block_state(state, last_seg, c, kb, vb, sb), out)
    init = (jnp.zeros((width, width), jnp.float32), jnp.int32(0))
    _, outs = lax.scan(step, init, xs)
    return outs.reshape(length, width)

def divergence_terms(new_logits, old_logits):
    lp_new = new_logits - jnp.log(lax.optimization_barrier(jnp.sum(jnp.exp(new_logits), axis=1, keepdims=True)))
    lp_old = old_logits - jnp.log(lax.optimization_barrier(jnp.sum(jnp.exp(old_logits), axis=1, keepdims=True)))
    return jnp.sum(jnp.exp(lp_old) * (lp_old - lp_new))

def reference(queries, keys, values, log_decay, starts, norm_gain, router_new, router_old):

    def one_slab(item):
        qs, ks, vs, ds, st = item
        positions = jnp.arange(SLAB_TOKENS, dtype=jnp.int32)
        seg = (lax.optimization_barrier(jnp.sum((st[None, :] <= positions[:, None]).astype(jnp.int32), axis=1)) - 1).astype(jnp.int32)

        def one_head(head):
            offset = (head * HD).astype(jnp.int32)
            qh = lax.dynamic_slice_in_dim(qs, offset, HD, 1)
            kh = lax.dynamic_slice_in_dim(ks, offset, HD, 1)
            vh = lax.dynamic_slice_in_dim(vs, offset, HD, 1)
            decay_lambda = lax.dynamic_slice_in_dim(ds, head.astype(jnp.int32), 1, 1)[:, 0].astype(jnp.float32)
            gain = lax.dynamic_slice_in_dim(norm_gain, offset, HD, 0)
            return head_attention(qh, kh, vh, decay_lambda, seg, gain, BLOCK)
        outs = lax.map(one_head, jnp.arange(HEADS, dtype=jnp.int32))
        normed = jnp.transpose(outs, (1, 0, 2)).reshape(SLAB_TOKENS, HEADS * HD)
        new_logits = jnp.dot(normed, router_new, preferred_element_type=jnp.float32)
        old_logits = jnp.dot(normed, router_old, preferred_element_type=jnp.float32)
        return (new_logits, divergence_terms(new_logits, old_logits))
    logits_new, sums = lax.map(one_slab, (queries, keys, values, log_decay, starts))
    return (logits_new, jnp.sum(sums) / (ROLLOUT_SLABS * SLAB_TOKENS))
```

```python
import functools

import jax
import jax.numpy as jnp
from jax import lax
from jax.experimental import pallas as pl
from jax.experimental.pallas import tpu as pltpu
from jax.sharding import PartitionSpec as P

MESH = pl.DeviceIdType.MESH
F32 = jnp.float32
BF16 = jnp.bfloat16
NEG = -1e30
LAG = 2
Z_CHIPS = 8


def split_two(x):
    hi = x.astype(BF16)
    return hi, (x - hi.astype(F32)).astype(BF16)


def body(
    n_dp, n_chips, n_z, n_tokens,
    starts_ref, lam_ref, gain_ref, rnew_hbm, rold_hbm, q_hbm, k_hbm, v_hbm,
    logits_ref, div_ref,
    q_buf, k_buf, v_buf, rn_buf, ro_buf, intra_buf,
    c_buf, ct_buf, tail_buf, carried_buf, mask_buf,
    a_own, a_sib, w_own, w_recv, a_chip, a_all,
    s_own, s_send, s_recv, fwd_send, fwd_recv, ret_send, ret_recv,
    p_send, p_buf, acc_buf, red_mine, red_plane, red_part, red_all,
    load_sem, a_sems, ach_ssem, ach_rsem, s_ssem, s_rsem, fwd_ssem, fwd_rsem,
    ret_ssem, ret_rsem, p_ssem, p_rsem, plane_ssem, plane_rsem, all_ssem, all_rsem,
):
    tok, width = q_hbm.shape
    hd = gain_ref.shape[1]
    pair = 2 * hd
    n_y = n_chips // n_z
    dp = lax.axis_index("dp")
    me = lax.axis_index("ctx")
    chip = lax.div(me, 2)
    core = lax.rem(me, 2)
    my_y = lax.div(chip, n_z)
    my_z = lax.rem(chip, n_z)
    sib = 2 * chip + (1 - core)

    def chip_at(i, sign):
        dy = lax.div(i, n_z)
        dz = lax.rem(i, n_z)
        if sign < 0:
            dy, dz = n_y - dy, n_z - dz
        return lax.rem(my_y + dy, n_y) * n_z + lax.rem(my_z + dz, n_z)

    def remote(src, dst, ssem, rsem, dp_to, ctx_to):
        return pltpu.make_async_remote_copy(
            src_ref=src, dst_ref=dst, send_sem=ssem, recv_sem=rsem,
            device_id=(dp_to, ctx_to), device_id_type=MESH,
        )

    barrier = pltpu.get_barrier_semaphore()

    def greet_chip(i, carry):
        pl.semaphore_signal(barrier, inc=1, device_id=(dp, 2 * chip_at(i, 1) + core), device_id_type=MESH)
        return carry

    lax.fori_loop(1, n_chips, greet_chip, 0)
    me8 = 2 * dp + core
    n_all = 2 * n_dp

    def all_peer(i):
        other = lax.rem(me8 + i, n_all)
        return lax.div(other, 2), 2 * chip + lax.rem(other, 2)

    def greet_all(i, carry):
        pl.semaphore_signal(barrier, inc=1, device_id=all_peer(i), device_id_type=MESH)
        return carry

    lax.fori_loop(1, n_all, greet_all, 0)

    part = width // n_y

    def load_part(j):
        cols = pl.ds(pl.multiple_of(lax.rem(my_y + j, n_y) * part, part), part)
        return (
            pltpu.make_async_copy(k_hbm.at[:, cols], k_buf.at[:, cols], load_sem.at[2 * j]),
            pltpu.make_async_copy(v_hbm.at[:, cols], v_buf.at[:, cols], load_sem.at[2 * j + 1]),
        )

    for j in range(n_y):
        for copy in load_part(j):
            copy.start()
    late = (
        pltpu.make_async_copy(q_hbm, q_buf, load_sem.at[2 * n_y]),
        pltpu.make_async_copy(rnew_hbm, rn_buf, load_sem.at[2 * n_y + 1]),
        pltpu.make_async_copy(rold_hbm, ro_buf, load_sem.at[2 * n_y + 2]),
    )
    for copy in late:
        copy.start()

    base = me * tok
    n_seg = starts_ref.shape[1]

    def segment(pos):
        seg = (starts_ref[0, 0] <= pos).astype(jnp.int32)
        for j in range(1, n_seg):
            seg = seg + (starts_ref[0, j] <= pos).astype(jnp.int32)
        return seg

    seg_col = segment(base + lax.broadcasted_iota(jnp.int32, (tok, 1), 0))
    seg_row = segment(base + lax.broadcasted_iota(jnp.int32, (1, tok), 1))
    seg_before = segment(base - 1 + lax.broadcasted_iota(jnp.int32, (1, 1), 1))
    seg_end = segment(base + tok - 1 + lax.broadcasted_iota(jnp.int32, (1, 1), 1))
    later = lax.broadcasted_iota(jnp.int32, (tok, tok), 0)
    earlier = lax.broadcasted_iota(jnp.int32, (tok, tok), 1)
    mask_buf[...] = jnp.where((later >= earlier) & (seg_col == seg_row), 0.0, NEG)
    tri = (later >= earlier).astype(BF16)
    lam = lam_ref[...]
    lam = jnp.concatenate([lam, jnp.zeros((tok, 128 - lam.shape[1]), BF16)], axis=1)
    c = jnp.dot(tri, lam, preferred_element_type=F32)
    c_buf[...] = c
    carried_buf[...] = jnp.exp(c) * (seg_col == seg_before).astype(F32)
    ct = c.T
    ct_buf[...] = ct
    total_c = ct[:, tok - 1 : tok]
    tail_buf[...] = jnp.exp(total_c - ct) * (seg_row == seg_end).astype(F32)
    decay = jnp.exp(total_c) * (seg_end == seg_before).astype(F32)
    decay = jnp.broadcast_to(decay, (ct.shape[0], 128))
    a_own[...] = decay

    pl.semaphore_wait(barrier, n_chips - 1 + n_all - 1)

    a_copy = remote(a_own, a_sib, a_sems.at[0], a_sems.at[1], dp, sib)
    a_copy.start()

    def swap_decays():
        a_copy.wait()
        own, other = a_own[...], a_sib[...]
        w_own[...] = jnp.where(core == 0, other, 1.0)
        w_recv[...] = jnp.where(core == 0, 1.0, own)
        both = own * other
        for h in range(2 * n_chips):
            a_chip[h] = both[h : h + 1, :]

    def s_copy(slot):
        return remote(s_send.at[slot], s_recv.at[slot], s_ssem.at[slot], s_rsem.at[slot], dp, sib)

    def fwd_copies(slot):
        to = 2 * slot + core
        return (
            remote(fwd_send.at[slot], fwd_recv.at[chip], fwd_ssem.at[slot], fwd_rsem.at[chip], dp, to),
            remote(a_chip.at[to], a_all.at[chip], ach_ssem.at[slot], ach_rsem.at[chip], dp, to),
        )

    def state_of(h):
        cols = pl.ds(pl.multiple_of(h * hd, hd), hd)
        kt = k_buf[:, cols].astype(F32).T * tail_buf[pl.ds(h, 1), :]
        hi, lo = split_two(kt)
        vh = v_buf[:, cols]
        return jnp.dot(hi, vh, preferred_element_type=F32) + jnp.dot(lo, vh, preferred_element_type=F32)

    def phase_one(i, carry):
        for j in range(n_y):
            @pl.when(i == j * n_z)
            def _():
                for copy in load_part(j):
                    copy.wait()

        @pl.when(i < n_chips)
        def _():
            slot = chip_at(i, 1)
            s_send[slot] = state_of(2 * slot + 1 - core)
            s_copy(slot).start()
            s_own[slot] = state_of(2 * slot + core)

        @pl.when(i == LAG)
        def _():
            swap_decays()

        @pl.when(i >= LAG)
        def _():
            slot = chip_at(i - LAG, 1)
            h = 2 * slot + core
            s_copy(slot).wait_recv()
            both = w_own[pl.ds(h, 1), :] * s_own[slot] + w_recv[pl.ds(h, 1), :] * s_recv[slot]

            @pl.when(slot != chip)
            def _():
                fwd_send[slot] = both.astype(BF16)
                for copy in fwd_copies(slot):
                    copy.start()

            @pl.when(slot == chip)
            def _():
                fwd_recv[slot] = both.astype(BF16)
                a_all[slot] = a_chip[h]

        return carry

    lax.fori_loop(0, n_chips + LAG, phase_one, 0)

    late[0].wait()

    def phase_two(i, carry):
        for half in range(2):
            h = 2 * i + half
            cols = pl.ds(pl.multiple_of(h * hd, hd), hd)
            scores = lax.dot_general(
                q_buf[:, cols], k_buf[:, cols], (((1,), (1,)), ((), ())), preferred_element_type=F32
            )
            c_col = pltpu.roll(c_buf[...], lax.rem(128 - h, 128), 1)[:, 0:1]
            weight = jnp.exp(c_col - ct_buf[pl.ds(h, 1), :] + mask_buf[...])
            probs = (scores * weight).astype(BF16)
            intra_buf[:, cols] = jnp.dot(probs, v_buf[:, cols], preferred_element_type=F32)
        return carry

    lax.fori_loop(0, n_chips, phase_two, 0)

    def scan_step(src, state):
        @pl.when(src != chip)
        def _():
            to = 2 * src + core
            remote(fwd_send.at[src], fwd_recv.at[src], fwd_ssem.at[src], fwd_rsem.at[src], dp, to).wait_recv()
            remote(a_chip.at[to], a_all.at[src], ach_ssem.at[src], ach_rsem.at[src], dp, to).wait_recv()

        ret_send[src] = state.astype(BF16)
        return a_all[src] * state + fwd_recv[src].astype(F32)

    lax.fori_loop(0, n_chips, scan_step, jnp.zeros((hd, hd), F32))

    def ret_copy(slot):
        return remote(
            ret_send.at[slot], ret_recv.at[chip], ret_ssem.at[slot], ret_rsem.at[chip], dp, 2 * slot + core
        )

    def send_back(i, carry):
        ret_copy(chip_at(i, 1)).start()
        return carry

    lax.fori_loop(1, n_chips, send_back, 0)
    ret_recv[chip] = ret_send[chip]
    late[1].wait()
    late[2].wait()
    acc_buf[...] = jnp.zeros_like(acc_buf)

    def p_copy(slot):
        return remote(p_send.at[slot], p_buf.at[slot, core], p_ssem.at[slot], p_rsem.at[slot], dp, sib)

    def head_out(slot, half):
        h = 2 * slot + half
        cols = pl.ds(pl.multiple_of(h * hd, hd), hd)
        hi, lo = split_two(p_buf[slot, half])
        qh = q_buf[:, cols]
        inter = jnp.dot(qh, hi, preferred_element_type=F32) + jnp.dot(qh, lo, preferred_element_type=F32)
        carried = pltpu.roll(carried_buf[...], lax.rem(128 - h, 128), 1)[:, 0:1]
        total = intra_buf[:, cols] + carried * inter
        meansq = jnp.mean(total * total, axis=1, keepdims=True) + 1e-06
        return split_two(total * lax.rsqrt(meansq) * gain_ref[pl.ds(h, 1), :])

    def phase_three(i, carry):
        @pl.when(i < n_chips)
        def _():
            slot = chip_at(i, -1)
            h = 2 * slot + core

            @pl.when(i > 0)
            def _():
                remote(
                    ret_send.at[slot], ret_recv.at[slot], ret_ssem.at[slot], ret_rsem.at[slot], dp, 2 * slot + core
                ).wait_recv()

            first = ret_recv[slot].astype(F32)

            @pl.when(core == 0)
            def _():
                p_buf[slot, core] = first
                p_send[slot] = a_own[pl.ds(h, 1), :] * first + s_own[slot]

            @pl.when(core == 1)
            def _():
                p_send[slot] = first
                p_buf[slot, core] = a_sib[pl.ds(h, 1), :] * first + s_recv[slot]

            p_copy(slot).start()

        @pl.when(i >= LAG)
        def _():
            slot = chip_at(i - LAG, -1)
            remote(
                p_send.at[slot], p_buf.at[slot, 1 - core], p_ssem.at[slot], p_rsem.at[slot], dp, sib
            ).wait_recv()
            hi0, lo0 = head_out(slot, 0)
            hi1, lo1 = head_out(slot, 1)
            rows = pl.ds(pl.multiple_of(slot * pair, pair), pair)
            weights = jnp.concatenate([rn_buf[rows, :], ro_buf[rows, :]], axis=1)
            hi = jnp.concatenate([hi0, hi1], axis=1)
            lo = jnp.concatenate([lo0, lo1], axis=1)
            acc_buf[...] += jnp.dot(hi, weights, preferred_element_type=F32) + jnp.dot(
                lo, weights, preferred_element_type=F32
            )

        return carry

    lax.fori_loop(0, n_chips + LAG, phase_three, 0)

    n_exp = logits_ref.shape[1]
    new = acc_buf[:, 0:n_exp]
    old = acc_buf[:, n_exp : 2 * n_exp]
    logits_ref[...] = new
    lp_new = new - jnp.log(jnp.sum(jnp.exp(new), axis=1, keepdims=True))
    lp_old = old - jnp.log(jnp.sum(jnp.exp(old), axis=1, keepdims=True))
    term = jnp.sum(jnp.exp(lp_old) * (lp_old - lp_new), axis=1, keepdims=True)
    mine = jnp.broadcast_to(jnp.sum(term, axis=0, keepdims=True), (1, 128))
    red_mine[...] = mine

    def plane_copy(slot):
        return remote(
            red_mine, red_plane.at[chip], plane_ssem.at[slot], plane_rsem.at[chip], dp, 2 * slot + core
        )

    def send_plane(i, carry):
        plane_copy(chip_at(i, 1)).start()
        return carry

    lax.fori_loop(1, n_chips, send_plane, 0)
    red_plane[chip] = mine

    def add_plane(src, total):
        @pl.when(src != chip)
        def _():
            remote(
                red_mine, red_plane.at[src], plane_ssem.at[src], plane_rsem.at[src], dp, 2 * src + core
            ).wait_recv()

        return total + red_plane[src]

    plane = lax.fori_loop(0, n_chips, add_plane, jnp.zeros((1, 128), F32))
    red_part[...] = plane

    def all_copy(i):
        return remote(red_part, red_all.at[me8], all_ssem.at[i], all_rsem.at[me8], *all_peer(i))

    for i in range(1, n_all):
        all_copy(i).start()
    red_all[me8] = plane
    total = jnp.zeros((1, 128), F32)
    for src in range(n_all):
        @pl.when(src != me8)
        def _():
            remote(
                red_part, red_all.at[src], all_ssem.at[src], all_rsem.at[src], src // 2, 2 * chip + src % 2
            ).wait_recv()

        total = total + red_all[src]
    div_ref[...] = total / n_tokens

    a_done = 0

    def sent(i, carry):
        slot = chip_at(i, 1)
        s_copy(slot).wait_send()
        p_copy(slot).wait_send()

        @pl.when(i > 0)
        def _():
            for copy in fwd_copies(slot):
                copy.wait_send()
            ret_copy(slot).wait_send()
            plane_copy(slot).wait_send()

        return carry

    lax.fori_loop(0, n_chips, sent, a_done)
    for i in range(1, n_all):
        all_copy(i).wait_send()


def local(queries, keys, values, log_decay, starts, norm_gain, router_new, router_old):
    _, tok, width = queries.shape
    heads = log_decay.shape[2]
    hd = width // heads
    n_ctx = lax.axis_size("ctx")
    n_dp = lax.axis_size("dp")
    n_chips = n_ctx // 2
    n_z = min(Z_CHIPS, n_chips)
    n_y = n_chips // n_z
    n_exp = router_new.shape[1]
    vmem = pltpu.VMEM
    dma = pltpu.SemaphoreType.DMA
    any_spec = pl.BlockSpec(memory_space=pl.ANY)
    vmem_spec = pl.BlockSpec(memory_space=pltpu.VMEM)
    logits, div = pl.pallas_call(
        functools.partial(body, n_dp, n_chips, n_z, tok * n_ctx * n_dp),
        out_shape=(
            jax.ShapeDtypeStruct((tok, n_exp), F32),
            jax.ShapeDtypeStruct((1, 128), F32),
        ),
        in_specs=[
            pl.BlockSpec(memory_space=pltpu.SMEM), vmem_spec, vmem_spec,
            any_spec, any_spec, any_spec, any_spec, any_spec,
        ],
        out_specs=(vmem_spec, vmem_spec),
        scratch_shapes=[
            vmem((tok, width), BF16), vmem((tok, width), BF16), vmem((tok, width), BF16),
            vmem((width, n_exp), BF16), vmem((width, n_exp), BF16), vmem((tok, width), F32),
            vmem((tok, 128), F32), vmem((128, tok), F32), vmem((128, tok), F32), vmem((tok, 128), F32),
            vmem((tok, tok), F32),
            vmem((128, 128), F32), vmem((128, 128), F32), vmem((128, 128), F32), vmem((128, 128), F32),
            vmem((2 * n_chips, 1, 128), F32), vmem((n_chips, 1, 128), F32),
            vmem((n_chips, hd, hd), F32), vmem((n_chips, hd, hd), F32), vmem((n_chips, hd, hd), F32),
            vmem((n_chips, hd, hd), BF16), vmem((n_chips, hd, hd), BF16),
            vmem((n_chips, hd, hd), BF16), vmem((n_chips, hd, hd), BF16),
            vmem((n_chips, hd, hd), F32), vmem((n_chips, 2, hd, hd), F32),
            vmem((tok, 2 * n_exp), F32),
            vmem((1, 128), F32), vmem((n_chips, 1, 128), F32), vmem((1, 128), F32),
            vmem((2 * n_dp, 1, 128), F32),
            dma((2 * n_y + 3,)), dma((2,)), dma((n_chips,)), dma((n_chips,)), dma((n_chips,)), dma((n_chips,)),
            dma((n_chips,)), dma((n_chips,)), dma((n_chips,)), dma((n_chips,)), dma((n_chips,)), dma((n_chips,)),
            dma((n_chips,)), dma((n_chips,)), dma((2 * n_dp,)), dma((2 * n_dp,)),
        ],
        compiler_params=pltpu.CompilerParams(
            collective_id=0, has_side_effects=True, vmem_limit_bytes=50 * 1024 * 1024
        ),
        name="attention_router",
    )(
        starts, log_decay[0], norm_gain.reshape(heads, hd), router_new, router_old,
        queries[0], keys[0], values[0],
    )
    return logits[None], div[0, 0]


def solution(mesh):
    in_specs = (
        P("dp", "ctx", None),
        P("dp", "ctx", None),
        P("dp", "ctx", None),
        P("dp", "ctx", None),
        P("dp", None),
        P(),
        P(),
        P(),
    )
    out_specs = (P("dp", "ctx", None), P())
    return jax.shard_map(local, mesh=mesh, in_specs=in_specs, out_specs=out_specs, check_vma=False)
```

```python
import functools

import jax
import jax.numpy as jnp
from jax import lax
from jax.experimental import pallas as pl
from jax.experimental.pallas import tpu as pltpu
from jax.sharding import PartitionSpec as P

MESH = pl.DeviceIdType.MESH
F32 = jnp.float32
BF16 = jnp.bfloat16
NEG = -1e30
LAG = 2
JOIN_LAG = 4
Z_CHIPS = 8


def split_two(x):
    hi = x.astype(BF16)
    return hi, (x - hi.astype(F32)).astype(BF16)


def body(
    n_dp, n_chips, n_z, n_tokens,
    starts_hbm, lam_hbm, gain_hbm, rnew_hbm, rold_hbm, q_hbm, k_hbm, v_hbm,
    logits_ref, div_ref,
    starts_ref, lam_ref, gain_ref, q_buf, k_buf, v_buf, rn_buf, ro_buf, intra_buf,
    c_buf, ct_buf, tail_buf, carried_buf, mask_buf,
    a_own, a_sib, w_own, w_recv, a_chip, a_all,
    s_own, s_send, s_recv, fwd_send, fwd_recv, ret_send, ret_recv,
    p_send, p_buf, acc_buf, red_mine, red_plane, red_part, red_all,
    load_sem, a_sems, ach_ssem, ach_rsem, s_ssem, s_rsem, fwd_ssem, fwd_rsem,
    ret_ssem, ret_rsem, p_ssem, p_rsem, plane_ssem, plane_rsem, all_ssem, all_rsem,
):
    tok, width = q_hbm.shape
    hd = gain_ref.shape[1]
    heads = gain_ref.shape[0]
    pair = 2 * hd
    n_y = n_chips // n_z
    dp = lax.axis_index("dp")
    me = lax.axis_index("ctx")
    chip = lax.div(me, 2)
    core = lax.rem(me, 2)
    my_y = lax.div(chip, n_z)
    my_z = lax.rem(chip, n_z)
    sib = 2 * chip + (1 - core)

    def chip_at(i, sign):
        dy = lax.div(i, n_z)
        dz = lax.rem(i, n_z)
        if sign < 0:
            dy, dz = n_y - dy, n_z - dz
        return lax.rem(my_y + dy, n_y) * n_z + lax.rem(my_z + dz, n_z)

    def remote(src, dst, ssem, rsem, dp_to, ctx_to):
        return pltpu.make_async_remote_copy(
            src_ref=src, dst_ref=dst, send_sem=ssem, recv_sem=rsem,
            device_id=(dp_to, ctx_to), device_id_type=MESH,
        )

    small = (
        pltpu.make_async_copy(starts_hbm, starts_ref, load_sem.at[2 * n_y + 3]),
        pltpu.make_async_copy(lam_hbm, lam_ref, load_sem.at[2 * n_y + 4]),
        pltpu.make_async_copy(gain_hbm, gain_ref, load_sem.at[2 * n_y + 5]),
    )
    for copy in small:
        copy.start()

    part = width // n_y

    def load_part(j):
        cols = pl.ds(pl.multiple_of(lax.rem(my_y + j, n_y) * part, part), part)
        return (
            pltpu.make_async_copy(k_hbm.at[:, cols], k_buf.at[:, cols], load_sem.at[2 * j]),
            pltpu.make_async_copy(v_hbm.at[:, cols], v_buf.at[:, cols], load_sem.at[2 * j + 1]),
        )

    for copy in load_part(0):
        copy.start()

    barrier = pltpu.get_barrier_semaphore()
    rows_of = [lax.rem(my_y + dy, n_y) * n_z for dy in range(n_y)]
    places = [lax.rem(my_z + dz, n_z) for dz in range(n_z)]
    for dy in range(n_y):
        for dz in range(n_z):
            if dy or dz:
                to = 2 * (rows_of[dy] + places[dz]) + core
                pl.semaphore_signal(barrier, inc=1, device_id=(dp, to), device_id_type=MESH)
    me8 = 2 * dp + core
    n_all = 2 * n_dp

    def all_peer(i):
        to_core = core if i % 2 == 0 else 1 - core
        return lax.rem(dp + i // 2, n_dp), 2 * chip + to_core

    for i in range(1, n_all):
        pl.semaphore_signal(barrier, inc=1, device_id=all_peer(i), device_id_type=MESH)

    late = (
        pltpu.make_async_copy(q_hbm, q_buf, load_sem.at[2 * n_y]),
        pltpu.make_async_copy(rnew_hbm, rn_buf, load_sem.at[2 * n_y + 1]),
        pltpu.make_async_copy(rold_hbm, ro_buf, load_sem.at[2 * n_y + 2]),
    )

    for copy in small:
        copy.wait()

    base = me * tok
    n_seg = starts_ref.shape[1]

    def segment(pos):
        seg = (starts_ref[0, 0] <= pos).astype(jnp.int32)
        for j in range(1, n_seg):
            seg = seg + (starts_ref[0, j] <= pos).astype(jnp.int32)
        return seg

    seg_col = segment(base + lax.broadcasted_iota(jnp.int32, (tok, 1), 0))
    seg_row = segment(base + lax.broadcasted_iota(jnp.int32, (1, tok), 1))
    seg_before = segment(base - 1 + lax.broadcasted_iota(jnp.int32, (1, 1), 1))
    seg_end = segment(base + tok - 1 + lax.broadcasted_iota(jnp.int32, (1, 1), 1))
    later = lax.broadcasted_iota(jnp.int32, (tok, tok), 0)
    earlier = lax.broadcasted_iota(jnp.int32, (tok, tok), 1)
    mask_buf[...] = jnp.where((later >= earlier) & (seg_col == seg_row), 0.0, NEG)
    until = (later <= earlier).astype(BF16)
    ct = jnp.dot(lam_ref[...], until, preferred_element_type=F32)
    ct_buf[...] = ct
    c = jnp.concatenate([ct, jnp.zeros((128 - heads, tok), F32)], axis=0).T
    c_buf[...] = c
    carried_buf[...] = jnp.exp(c) * (seg_col == seg_before).astype(F32)
    total_c = ct[:, tok - 1 : tok]
    tail_buf[...] = jnp.exp(total_c - ct) * (seg_row == seg_end).astype(F32)
    decay = jnp.exp(total_c) * (seg_end == seg_before).astype(F32)
    a_own[...] = jnp.broadcast_to(decay, (heads, 128))

    def state_of(h):
        cols = pl.ds(pl.multiple_of(h * hd, hd), hd)
        kt = k_buf[:, cols].astype(F32).T * tail_buf[pl.ds(h, 1), :]
        hi, lo = split_two(kt)
        vh = v_buf[:, cols]
        return jnp.dot(hi, vh, preferred_element_type=F32) + jnp.dot(lo, vh, preferred_element_type=F32)

    def add_states(i):
        for j in range(n_y):
            @pl.when(i == j * n_z)
            def _():
                for copy in load_part(j):
                    copy.wait()
                if j + 1 < n_y:
                    for copy in load_part(j + 1):
                        copy.start()
                else:
                    for copy in late:
                        copy.start()

        slot = chip_at(i, 1)
        s_send[slot] = state_of(2 * slot + 1 - core).astype(BF16)
        s_own[slot] = state_of(2 * slot + core)

    def s_copy(slot):
        return remote(s_send.at[slot], s_recv.at[slot], s_ssem.at[slot], s_rsem.at[slot], dp, sib)

    def fwd_copy(slot):
        return remote(
            fwd_send.at[slot], fwd_recv.at[chip], fwd_ssem.at[slot], fwd_rsem.at[chip], dp, 2 * slot + core
        )

    def ach_copy(slot):
        to = 2 * slot + core
        return remote(a_chip.at[to], a_all.at[chip], ach_ssem.at[slot], ach_rsem.at[chip], dp, to)

    def join(i):
        slot = chip_at(i, 1)
        h = 2 * slot + core
        s_copy(slot).wait_recv()
        joined = w_own[pl.ds(h, 1), :] * s_own[slot] + w_recv[pl.ds(h, 1), :] * s_recv[slot].astype(F32)

        @pl.when(i > 0)
        def _():
            fwd_send[slot] = joined.astype(BF16)
            fwd_copy(slot).start()
            ach_copy(slot).start()

        @pl.when(i == 0)
        def _():
            fwd_recv[slot] = joined.astype(BF16)
            a_all[slot] = a_chip[h]

    add_states(0)
    pl.semaphore_wait(barrier, n_chips - 1 + n_all - 1)
    a_copy = remote(a_own, a_sib, a_sems.at[0], a_sems.at[1], dp, sib)
    a_copy.start()
    s_copy(chip).start()

    def first_states(i, carry):
        add_states(i)
        s_copy(chip_at(i, 1)).start()
        return carry

    lax.fori_loop(1, JOIN_LAG, first_states, 0)
    a_copy.wait()
    own, other = a_own[...], a_sib[...]
    w_own[...] = jnp.where(core == 0, other, 1.0)
    w_recv[...] = jnp.where(core == 0, 1.0, own)
    both_decay = own * other
    for h in range(heads):
        a_chip[h] = both_decay[h : h + 1, :]

    def phase_one(i, carry):
        @pl.when(i < n_chips)
        def _():
            add_states(i)
            s_copy(chip_at(i, 1)).start()

        join(i - JOIN_LAG)
        return carry

    lax.fori_loop(JOIN_LAG, n_chips + JOIN_LAG, phase_one, 0)

    late[0].wait()

    def phase_two(i, carry):
        for half in range(2):
            h = 2 * i + half
            cols = pl.ds(pl.multiple_of(h * hd, hd), hd)
            scores = lax.dot_general(
                q_buf[:, cols], k_buf[:, cols], (((1,), (1,)), ((), ())), preferred_element_type=F32
            )
            c_col = pltpu.roll(c_buf[...], lax.rem(128 - h, 128), 1)[:, 0:1]
            weight = jnp.exp(c_col - ct_buf[pl.ds(h, 1), :] + mask_buf[...])
            probs = (scores * weight).astype(BF16)
            intra_buf[:, cols] = jnp.dot(probs, v_buf[:, cols], preferred_element_type=F32)
        return carry

    lax.fori_loop(0, n_chips, phase_two, 0)

    def scan_step(src, state):
        @pl.when(src != chip)
        def _():
            to = 2 * src + core
            remote(fwd_send.at[src], fwd_recv.at[src], fwd_ssem.at[src], fwd_rsem.at[src], dp, to).wait_recv()
            remote(a_chip.at[to], a_all.at[src], ach_ssem.at[src], ach_rsem.at[src], dp, to).wait_recv()

        ret_send[src] = state.astype(BF16)
        return a_all[src] * state + fwd_recv[src].astype(F32)

    lax.fori_loop(0, n_chips, scan_step, jnp.zeros((hd, hd), F32))

    def ret_copy(slot):
        return remote(
            ret_send.at[slot], ret_recv.at[chip], ret_ssem.at[slot], ret_rsem.at[chip], dp, 2 * slot + core
        )

    def send_back(i, carry):
        ret_copy(chip_at(i, 1)).start()
        return carry

    lax.fori_loop(1, n_chips, send_back, 0)
    ret_recv[chip] = ret_send[chip]
    late[1].wait()
    late[2].wait()
    acc_buf[...] = jnp.zeros_like(acc_buf)

    def p_copy(slot):
        return remote(p_send.at[slot], p_buf.at[slot, core], p_ssem.at[slot], p_rsem.at[slot], dp, sib)

    def head_out(slot, half):
        h = 2 * slot + half
        cols = pl.ds(pl.multiple_of(h * hd, hd), hd)
        hi, lo = split_two(p_buf[slot, half])
        qh = q_buf[:, cols]
        inter = jnp.dot(qh, hi, preferred_element_type=F32) + jnp.dot(qh, lo, preferred_element_type=F32)
        carried = pltpu.roll(carried_buf[...], lax.rem(128 - h, 128), 1)[:, 0:1]
        total = intra_buf[:, cols] + carried * inter
        meansq = jnp.mean(total * total, axis=1, keepdims=True) + 1e-06
        return split_two(total * lax.rsqrt(meansq) * gain_ref[pl.ds(h, 1), :])

    def phase_three(i, carry):
        @pl.when(i < n_chips)
        def _():
            slot = chip_at(i, -1)
            h = 2 * slot + core

            @pl.when(i > 0)
            def _():
                remote(
                    ret_send.at[slot], ret_recv.at[slot], ret_ssem.at[slot], ret_rsem.at[slot], dp, 2 * slot + core
                ).wait_recv()

            first = ret_recv[slot].astype(F32)

            @pl.when(core == 0)
            def _():
                p_buf[slot, core] = first
                p_send[slot] = a_own[pl.ds(h, 1), :] * first + s_own[slot]

            @pl.when(core == 1)
            def _():
                p_send[slot] = first
                p_buf[slot, core] = a_sib[pl.ds(h, 1), :] * first + s_recv[slot].astype(F32)

            p_copy(slot).start()

        @pl.when(i >= LAG)
        def _():
            slot = chip_at(i - LAG, -1)
            remote(
                p_send.at[slot], p_buf.at[slot, 1 - core], p_ssem.at[slot], p_rsem.at[slot], dp, sib
            ).wait_recv()
            hi0, lo0 = head_out(slot, 0)
            hi1, lo1 = head_out(slot, 1)
            cols = pl.ds(pl.multiple_of(slot * pair, pair), pair)
            weights = jnp.concatenate([rn_buf[:, cols], ro_buf[:, cols]], axis=0)
            hi = jnp.concatenate([hi0, hi1], axis=1)
            lo = jnp.concatenate([lo0, lo1], axis=1)
            for x in (hi, lo):
                acc_buf[...] += lax.dot_general(
                    x, weights, (((1,), (1,)), ((), ())), preferred_element_type=F32
                )

        return carry

    lax.fori_loop(0, n_chips + LAG, phase_three, 0)

    n_exp = logits_ref.shape[0]
    both_logits = acc_buf[...].T
    new = both_logits[0:n_exp, :]
    old = both_logits[n_exp:, :]
    logits_ref[...] = new
    lp_new = new - jnp.log(jnp.sum(jnp.exp(new), axis=0, keepdims=True))
    lp_old = old - jnp.log(jnp.sum(jnp.exp(old), axis=0, keepdims=True))
    term = jnp.sum(jnp.exp(lp_old) * (lp_old - lp_new), axis=0, keepdims=True)
    mine = jnp.broadcast_to(jnp.sum(term, axis=1, keepdims=True), (1, 128))
    red_mine[...] = mine

    def plane_copy(slot):
        return remote(
            red_mine, red_plane.at[chip], plane_ssem.at[slot], plane_rsem.at[chip], dp, 2 * slot + core
        )

    def send_plane(i, carry):
        plane_copy(chip_at(i, 1)).start()
        return carry

    lax.fori_loop(1, n_chips, send_plane, 0)
    red_plane[chip] = mine

    def add_plane(src, total):
        @pl.when(src != chip)
        def _():
            remote(
                red_mine, red_plane.at[src], plane_ssem.at[src], plane_rsem.at[src], dp, 2 * src + core
            ).wait_recv()

        return total + red_plane[src]

    plane = lax.fori_loop(0, n_chips, add_plane, jnp.zeros((1, 128), F32))
    red_part[...] = plane

    def all_copy(i):
        return remote(red_part, red_all.at[me8], all_ssem.at[i], all_rsem.at[me8], *all_peer(i))

    for i in range(1, n_all):
        all_copy(i).start()
    red_all[me8] = plane
    total = jnp.zeros((1, 128), F32)
    for src in range(n_all):
        @pl.when(src != me8)
        def _():
            remote(
                red_part, red_all.at[src], all_ssem.at[src], all_rsem.at[src], src // 2, 2 * chip + src % 2
            ).wait_recv()

        total = total + red_all[src]
    div_ref[...] = total / n_tokens

    def sent(i, carry):
        slot = chip_at(i, 1)
        s_copy(slot).wait_send()
        p_copy(slot).wait_send()

        @pl.when(i > 0)
        def _():
            fwd_copy(slot).wait_send()
            ret_copy(slot).wait_send()
            ach_copy(slot).wait_send()
            plane_copy(slot).wait_send()

        return carry

    lax.fori_loop(0, n_chips, sent, 0)
    for i in range(1, n_all):
        all_copy(i).wait_send()


def local(queries, keys, values, log_decay, starts, norm_gain, router_new, router_old):
    _, tok, width = queries.shape
    heads = log_decay.shape[2]
    hd = width // heads
    n_ctx = lax.axis_size("ctx")
    n_dp = lax.axis_size("dp")
    n_chips = n_ctx // 2
    n_z = min(Z_CHIPS, n_chips)
    n_y = n_chips // n_z
    n_exp = router_new.shape[1]
    vmem = pltpu.VMEM
    dma = pltpu.SemaphoreType.DMA
    hbm_spec = pl.BlockSpec(memory_space=pltpu.HBM)
    vmem_spec = pl.BlockSpec(memory_space=pltpu.VMEM)
    logits, div = pl.pallas_call(
        functools.partial(body, n_dp, n_chips, n_z, tok * n_ctx * n_dp),
        out_shape=(
            jax.ShapeDtypeStruct((n_exp, tok), F32),
            jax.ShapeDtypeStruct((1, 128), F32),
        ),
        in_specs=[
            hbm_spec, hbm_spec, hbm_spec, hbm_spec, hbm_spec, hbm_spec, hbm_spec, hbm_spec,
        ],
        out_specs=(vmem_spec, vmem_spec),
        scratch_shapes=[
            pltpu.SMEM(starts.shape, starts.dtype), vmem((heads, tok), BF16), vmem((heads, hd), F32),
            vmem((tok, width), BF16), vmem((tok, width), BF16), vmem((tok, width), BF16),
            vmem((n_exp, width), BF16), vmem((n_exp, width), BF16), vmem((tok, width), F32),
            vmem((tok, 128), F32), vmem((heads, tok), F32), vmem((heads, tok), F32), vmem((tok, 128), F32),
            vmem((tok, tok), F32),
            vmem((heads, 128), F32), vmem((heads, 128), F32), vmem((heads, 128), F32), vmem((heads, 128), F32),
            vmem((2 * n_chips, 1, 128), F32), vmem((n_chips, 1, 128), F32),
            vmem((n_chips, hd, hd), F32), vmem((n_chips, hd, hd), BF16), vmem((n_chips, hd, hd), BF16),
            vmem((n_chips, hd, hd), BF16), vmem((n_chips, hd, hd), BF16),
            vmem((n_chips, hd, hd), BF16), vmem((n_chips, hd, hd), BF16),
            vmem((n_chips, hd, hd), F32), vmem((n_chips, 2, hd, hd), F32),
            vmem((tok, 2 * n_exp), F32),
            vmem((1, 128), F32), vmem((n_chips, 1, 128), F32), vmem((1, 128), F32),
            vmem((2 * n_dp, 1, 128), F32),
            dma((2 * n_y + 6,)), dma((2,)), dma((n_chips,)), dma((n_chips,)), dma((n_chips,)), dma((n_chips,)),
            dma((n_chips,)), dma((n_chips,)), dma((n_chips,)), dma((n_chips,)),
            dma((n_chips,)), dma((n_chips,)),
            dma((n_chips,)), dma((n_chips,)), dma((2 * n_dp,)), dma((2 * n_dp,)),
        ],
        compiler_params=pltpu.CompilerParams(
            collective_id=0, has_side_effects=True, vmem_limit_bytes=50 * 1024 * 1024
        ),
        name="attention_router",
    )(
        starts, log_decay[0].T, norm_gain.reshape(heads, hd), router_new.T, router_old.T,
        queries[0], keys[0], values[0],
    )
    return logits.T[None], div[0, 0]


def solution(mesh):
    in_specs = (
        P("dp", "ctx", None),
        P("dp", "ctx", None),
        P("dp", "ctx", None),
        P("dp", "ctx", None),
        P("dp", None),
        P(),
        P(),
        P(),
    )
    out_specs = (P("dp", "ctx", None), P())
    return jax.shard_map(local, mesh=mesh, in_specs=in_specs, out_specs=out_specs, check_vma=False)
```

```python
import functools

import jax
import jax.numpy as jnp
from jax import lax
from jax.experimental import pallas as pl
from jax.experimental.pallas import tpu as pltpu
from jax.sharding import PartitionSpec as P

MESH = pl.DeviceIdType.MESH
F32 = jnp.float32
BF16 = jnp.bfloat16
NEG = -1e30
GROUP = 2
JOIN_LAG = 4
Z_CHIPS = 8


def split_two(x):
    hi = x.astype(BF16)
    return hi, (x - hi.astype(F32)).astype(BF16)


def body(
    n_dp, n_chips, n_z, n_tokens,
    starts_hbm, lam_hbm, gain_hbm, rnew_hbm, rold_hbm, q_hbm, k_hbm, v_hbm,
    logits_ref, div_ref,
    starts_ref, lam_ref, gain_ref, q_buf, k_buf, v_buf, rn_buf, ro_buf, intra_buf,
    c_buf, ct_buf, tail_buf, carried_buf, mask_buf,
    a_own, a_sib, w_own, w_recv, a_chip, a_all,
    s_own, s_send, s_recv, fwd_send, fwd_recv, ret_send, ret_recv,
    p_send, p_buf, acc_buf, red_mine, red_plane, red_part, red_all,
    load_sem, a_sems, ach_ssem, ach_rsem, s_ssem, s_rsem, fwd_ssem, fwd_rsem,
    ret_ssem, ret_rsem, p_ssem, p_rsem, plane_ssem, plane_rsem, all_ssem, all_rsem,
):
    tok, width = q_hbm.shape
    hd = gain_ref.shape[1]
    heads = gain_ref.shape[0]
    n_y = n_chips // n_z
    dp = lax.axis_index("dp")
    me = lax.axis_index("ctx")
    chip = lax.div(me, 2)
    core = lax.rem(me, 2)
    my_y = lax.div(chip, n_z)
    my_z = lax.rem(chip, n_z)
    sib = 2 * chip + (1 - core)

    def chip_at(i, sign):
        dy = lax.div(i, n_z)
        dz = lax.rem(i, n_z)
        if sign < 0:
            dy, dz = n_y - dy, n_z - dz
        return lax.rem(my_y + dy, n_y) * n_z + lax.rem(my_z + dz, n_z)

    def remote(src, dst, ssem, rsem, dp_to, ctx_to):
        return pltpu.make_async_remote_copy(
            src_ref=src, dst_ref=dst, send_sem=ssem, recv_sem=rsem,
            device_id=(dp_to, ctx_to), device_id_type=MESH,
        )

    part = width // n_y

    def load_part(j):
        cols = pl.ds(pl.multiple_of(lax.rem(my_y + j, n_y) * part, part), part)
        return (
            pltpu.make_async_copy(k_hbm.at[:, cols], k_buf.at[:, cols], load_sem.at[2 * j]),
            pltpu.make_async_copy(v_hbm.at[:, cols], v_buf.at[:, cols], load_sem.at[2 * j + 1]),
        )

    for copy in load_part(0):
        copy.start()
    small = (
        pltpu.make_async_copy(starts_hbm, starts_ref, load_sem.at[2 * n_y + 3]),
        pltpu.make_async_copy(lam_hbm, lam_ref, load_sem.at[2 * n_y + 4]),
        pltpu.make_async_copy(gain_hbm, gain_ref, load_sem.at[2 * n_y + 5]),
    )
    for copy in small:
        copy.start()

    barrier = pltpu.get_barrier_semaphore()
    rows_of = [lax.rem(my_y + dy, n_y) * n_z for dy in range(n_y)]
    places = [lax.rem(my_z + dz, n_z) for dz in range(n_z)]
    for dy in range(n_y):
        for dz in range(n_z):
            if dy or dz:
                to = 2 * (rows_of[dy] + places[dz]) + core
                pl.semaphore_signal(barrier, inc=1, device_id=(dp, to), device_id_type=MESH)
    me8 = 2 * dp + core
    n_all = 2 * n_dp

    def all_peer(i):
        to_core = core if i % 2 == 0 else 1 - core
        return lax.rem(dp + i // 2, n_dp), 2 * chip + to_core

    for i in range(1, n_all):
        pl.semaphore_signal(barrier, inc=1, device_id=all_peer(i), device_id_type=MESH)

    late = (
        pltpu.make_async_copy(q_hbm, q_buf, load_sem.at[2 * n_y]),
        pltpu.make_async_copy(rnew_hbm, rn_buf, load_sem.at[2 * n_y + 1]),
        pltpu.make_async_copy(rold_hbm, ro_buf, load_sem.at[2 * n_y + 2]),
    )

    for copy in small:
        copy.wait()

    base = me * tok
    n_seg = starts_ref.shape[1]

    def segment(pos):
        seg = (starts_ref[0, 0] <= pos).astype(jnp.int32)
        for j in range(1, n_seg):
            seg = seg + (starts_ref[0, j] <= pos).astype(jnp.int32)
        return seg

    seg_col = segment(base + lax.broadcasted_iota(jnp.int32, (tok, 1), 0))
    seg_row = segment(base + lax.broadcasted_iota(jnp.int32, (1, tok), 1))
    seg_before = segment(base - 1 + lax.broadcasted_iota(jnp.int32, (1, 1), 1))
    seg_end = segment(base + tok - 1 + lax.broadcasted_iota(jnp.int32, (1, 1), 1))
    later = lax.broadcasted_iota(jnp.int32, (tok, tok), 0)
    earlier = lax.broadcasted_iota(jnp.int32, (tok, tok), 1)
    mask_buf[...] = jnp.where((later >= earlier) & (seg_col == seg_row), 0.0, NEG)
    until = (later <= earlier).astype(BF16)
    ct = jnp.dot(lam_ref[...], until, preferred_element_type=F32)
    ct_buf[...] = ct
    c = jnp.concatenate([ct, jnp.zeros((128 - heads, tok), F32)], axis=0).T
    c_buf[...] = c
    carried_buf[...] = jnp.exp(c) * (seg_col == seg_before).astype(F32)
    total_c = ct[:, tok - 1 : tok]
    tail_buf[...] = jnp.exp(total_c - ct) * (seg_row == seg_end).astype(F32)
    decay = jnp.exp(total_c) * (seg_end == seg_before).astype(F32)
    a_own[...] = jnp.broadcast_to(decay, (heads, 128))

    def state_of(h):
        cols = pl.ds(pl.multiple_of(h * hd, hd), hd)
        kt = k_buf[:, cols].astype(F32).T * tail_buf[pl.ds(h, 1), :]
        hi, lo = split_two(kt)
        vh = v_buf[:, cols]
        return jnp.dot(hi, vh, preferred_element_type=F32) + jnp.dot(lo, vh, preferred_element_type=F32)

    def add_states(i):
        for j in range(n_y):
            @pl.when(i == j * n_z)
            def _():
                for copy in load_part(j):
                    copy.wait()
                if j + 1 < n_y:
                    for copy in load_part(j + 1):
                        copy.start()
                else:
                    for copy in late:
                        copy.start()

        slot = chip_at(i, 1)
        s_send[slot] = state_of(2 * slot + 1 - core).astype(BF16)
        s_own[slot] = state_of(2 * slot + core)

    def s_copy(slot):
        return remote(s_send.at[slot], s_recv.at[slot], s_ssem.at[slot], s_rsem.at[slot], dp, sib)

    def fwd_copy(slot):
        return remote(
            fwd_send.at[slot], fwd_recv.at[chip], fwd_ssem.at[slot], fwd_rsem.at[chip], dp, 2 * slot + core
        )

    def ach_copy(slot):
        to = 2 * slot + core
        return remote(a_chip.at[to], a_all.at[chip], ach_ssem.at[slot], ach_rsem.at[chip], dp, to)

    def join(i):
        slot = chip_at(i, 1)
        h = 2 * slot + core
        s_copy(slot).wait_recv()
        joined = w_own[pl.ds(h, 1), :] * s_own[slot] + w_recv[pl.ds(h, 1), :] * s_recv[slot].astype(F32)

        @pl.when(i > 0)
        def _():
            fwd_send[slot] = joined.astype(BF16)
            fwd_copy(slot).start()
            ach_copy(slot).start()

        @pl.when(i == 0)
        def _():
            fwd_recv[slot] = joined.astype(BF16)
            a_all[slot] = a_chip[h]

    add_states(0)
    pl.semaphore_wait(barrier, n_chips - 1 + n_all - 1)
    a_copy = remote(a_own, a_sib, a_sems.at[0], a_sems.at[1], dp, sib)
    a_copy.start()
    s_copy(chip).start()

    def first_states(i, carry):
        add_states(i)
        s_copy(chip_at(i, 1)).start()
        return carry

    lax.fori_loop(1, JOIN_LAG, first_states, 0)
    a_copy.wait()
    own, other = a_own[...], a_sib[...]
    w_own[...] = jnp.where(core == 0, other, 1.0)
    w_recv[...] = jnp.where(core == 0, 1.0, own)
    both_decay = own * other
    for h in range(heads):
        a_chip[h] = both_decay[h : h + 1, :]

    def phase_one(i, carry):
        @pl.when(i < n_chips)
        def _():
            add_states(i)
            s_copy(chip_at(i, 1)).start()

        join(i - JOIN_LAG)
        return carry

    lax.fori_loop(JOIN_LAG, n_chips + JOIN_LAG, phase_one, 0)

    late[0].wait()

    def phase_two(i, carry):
        for half in range(2):
            h = 2 * i + half
            cols = pl.ds(pl.multiple_of(h * hd, hd), hd)
            scores = lax.dot_general(
                q_buf[:, cols], k_buf[:, cols], (((1,), (1,)), ((), ())), preferred_element_type=F32
            )
            c_col = pltpu.roll(c_buf[...], lax.rem(128 - h, 128), 1)[:, 0:1]
            weight = jnp.exp(c_col - ct_buf[pl.ds(h, 1), :] + mask_buf[...])
            probs = (scores * weight).astype(BF16)
            intra_buf[:, cols] = jnp.dot(probs, v_buf[:, cols], preferred_element_type=F32)
        return carry

    lax.fori_loop(0, n_chips, phase_two, 0)

    def wait_states(i, carry):
        src = chip_at(i, -1)
        to = 2 * src + core
        remote(fwd_send.at[src], fwd_recv.at[src], fwd_ssem.at[src], fwd_rsem.at[src], dp, to).wait_recv()
        remote(a_chip.at[to], a_all.at[src], ach_ssem.at[src], ach_rsem.at[src], dp, to).wait_recv()
        return carry

    lax.fori_loop(1, n_chips, wait_states, 0)

    def scan_four(i, state):
        for j in range(4):
            src = 4 * i + j
            ret_send[src] = state.astype(BF16)
            state = a_all[src] * state + fwd_recv[src].astype(F32)
        return state

    lax.fori_loop(0, n_chips // 4, scan_four, jnp.zeros((hd, hd), F32))

    def ret_copy(slot):
        return remote(
            ret_send.at[slot], ret_recv.at[chip], ret_ssem.at[slot], ret_rsem.at[chip], dp, 2 * slot + core
        )

    def send_back(i, carry):
        ret_copy(chip_at(i, 1)).start()
        return carry

    lax.fori_loop(1, n_chips, send_back, 0)
    ret_recv[chip] = ret_send[chip]
    late[1].wait()
    late[2].wait()
    acc_buf[...] = jnp.zeros_like(acc_buf)

    def p_copy(slot):
        return remote(p_send.at[slot], p_buf.at[slot, core], p_ssem.at[slot], p_rsem.at[slot], dp, sib)

    def head_out(slot, half):
        h = 2 * slot + half
        cols = pl.ds(pl.multiple_of(h * hd, hd), hd)
        hi, lo = split_two(p_buf[slot, half])
        qh = q_buf[:, cols]
        inter = jnp.dot(qh, hi, preferred_element_type=F32) + jnp.dot(qh, lo, preferred_element_type=F32)
        carried = pltpu.roll(carried_buf[...], lax.rem(128 - h, 128), 1)[:, 0:1]
        total = intra_buf[:, cols] + carried * inter
        meansq = jnp.mean(total * total, axis=1, keepdims=True) + 1e-06
        return split_two(total * lax.rsqrt(meansq) * gain_ref[pl.ds(h, 1), :])

    def hand_over(i):
        slot = chip_at(i, -1)
        h = 2 * slot + core

        @pl.when(i > 0)
        def _():
            remote(
                ret_send.at[slot], ret_recv.at[slot], ret_ssem.at[slot], ret_rsem.at[slot], dp, 2 * slot + core
            ).wait_recv()

        first = ret_recv[slot].astype(F32)

        @pl.when(core == 0)
        def _():
            p_buf[slot, core] = first
            p_send[slot] = a_own[pl.ds(h, 1), :] * first + s_own[slot]

        @pl.when(core == 1)
        def _():
            p_send[slot] = first
            p_buf[slot, core] = a_sib[pl.ds(h, 1), :] * first + s_recv[slot].astype(F32)

        p_copy(slot).start()

    def phase_three(i, carry):
        @pl.when(i < n_chips // GROUP)
        def _():
            for j in range(GROUP):
                hand_over(i * GROUP + j)

        @pl.when(i > 0)
        def _():
            slots = [chip_at((i - 1) * GROUP + j, -1) for j in range(GROUP)]
            for slot in slots:
                remote(
                    p_send.at[slot], p_buf.at[slot, 1 - core], p_ssem.at[slot], p_rsem.at[slot], dp, sib
                ).wait_recv()
            outs = [[head_out(slot, half) for half in range(2)] for slot in slots]
            acc = acc_buf[...]
            for slot, (first, second) in zip(slots, outs):
                cols = pl.ds(pl.multiple_of(slot * 2 * hd, 2 * hd), 2 * hd)
                weights = jnp.concatenate([rn_buf[:, cols], ro_buf[:, cols]], axis=0)
                for x, y in zip(first, second):
                    acc = acc + lax.dot_general(
                        jnp.concatenate([x, y], axis=1), weights, (((1,), (1,)), ((), ())),
                        preferred_element_type=F32,
                    )
            acc_buf[...] = acc

        return carry

    lax.fori_loop(0, n_chips // GROUP + 1, phase_three, 0)

    n_exp = logits_ref.shape[0]
    both_logits = acc_buf[...].T
    new = both_logits[0:n_exp, :]
    old = both_logits[n_exp:, :]
    logits_ref[...] = new
    lp_new = new - jnp.log(jnp.sum(jnp.exp(new), axis=0, keepdims=True))
    lp_old = old - jnp.log(jnp.sum(jnp.exp(old), axis=0, keepdims=True))
    term = jnp.sum(jnp.exp(lp_old) * (lp_old - lp_new), axis=0, keepdims=True)
    mine = jnp.broadcast_to(jnp.sum(term, axis=1, keepdims=True), (1, 128))
    red_mine[...] = mine

    def plane_copy(dy, dz):
        i = dy * n_z + dz
        return remote(
            red_mine, red_plane.at[chip], plane_ssem.at[i], plane_rsem.at[i], dp,
            2 * (rows_of[dy] + places[dz]) + core,
        )

    plane_copies = [plane_copy(dy, dz) for dy in range(n_y) for dz in range(n_z) if dy or dz]
    for copy in plane_copies:
        copy.start()
    red_plane[chip] = mine

    def sent(i, carry):
        slot = chip_at(i, 1)
        s_copy(slot).wait_send()
        p_copy(slot).wait_send()

        @pl.when(i > 0)
        def _():
            fwd_copy(slot).wait_send()
            ret_copy(slot).wait_send()
            ach_copy(slot).wait_send()

        return carry

    lax.fori_loop(0, n_chips, sent, 0)
    for copy in plane_copies:
        copy.wait_recv()
    plane = jnp.sum(red_plane[...], axis=0)
    red_part[...] = plane

    def all_copy(i):
        return remote(red_part, red_all.at[me8], all_ssem.at[i], all_rsem.at[i], *all_peer(i))

    all_copies = [all_copy(i) for i in range(1, n_all)]
    for copy in all_copies:
        copy.start()
    red_all[me8] = plane
    for copy in plane_copies:
        copy.wait_send()
    for copy in all_copies:
        copy.wait()
    div_ref[...] = jnp.sum(red_all[...], axis=0) / n_tokens


def local(queries, keys, values, log_decay, starts, norm_gain, router_new, router_old):
    _, tok, width = queries.shape
    heads = log_decay.shape[2]
    hd = width // heads
    n_ctx = lax.axis_size("ctx")
    n_dp = lax.axis_size("dp")
    n_chips = n_ctx // 2
    n_z = min(Z_CHIPS, n_chips)
    n_y = n_chips // n_z
    n_exp = router_new.shape[1]
    vmem = pltpu.VMEM
    dma = pltpu.SemaphoreType.DMA
    hbm_spec = pl.BlockSpec(memory_space=pltpu.HBM)
    vmem_spec = pl.BlockSpec(memory_space=pltpu.VMEM)
    logits, div = pl.pallas_call(
        functools.partial(body, n_dp, n_chips, n_z, tok * n_ctx * n_dp),
        out_shape=(
            jax.ShapeDtypeStruct((n_exp, tok), F32),
            jax.ShapeDtypeStruct((1, 128), F32),
        ),
        in_specs=[
            hbm_spec, hbm_spec, hbm_spec, hbm_spec, hbm_spec, hbm_spec, hbm_spec, hbm_spec,
        ],
        out_specs=(vmem_spec, vmem_spec),
        scratch_shapes=[
            pltpu.SMEM(starts.shape, starts.dtype), vmem((heads, tok), BF16), vmem((heads, hd), F32),
            vmem((tok, width), BF16), vmem((tok, width), BF16), vmem((tok, width), BF16),
            vmem((n_exp, width), BF16), vmem((n_exp, width), BF16), vmem((tok, width), F32),
            vmem((tok, 128), F32), vmem((heads, tok), F32), vmem((heads, tok), F32), vmem((tok, 128), F32),
            vmem((tok, tok), F32),
            vmem((heads, 128), F32), vmem((heads, 128), F32), vmem((heads, 128), F32), vmem((heads, 128), F32),
            vmem((2 * n_chips, 1, 128), F32), vmem((n_chips, 1, 128), F32),
            vmem((n_chips, hd, hd), F32), vmem((n_chips, hd, hd), BF16), vmem((n_chips, hd, hd), BF16),
            vmem((n_chips, hd, hd), BF16), vmem((n_chips, hd, hd), BF16),
            vmem((n_chips, hd, hd), BF16), vmem((n_chips, hd, hd), BF16),
            vmem((n_chips, hd, hd), F32), vmem((n_chips, 2, hd, hd), F32),
            vmem((tok, 2 * n_exp), F32),
            vmem((1, 128), F32), vmem((n_chips, 1, 128), F32), vmem((1, 128), F32),
            vmem((2 * n_dp, 1, 128), F32),
            dma((2 * n_y + 6,)), dma((2,)), dma((n_chips,)), dma((n_chips,)), dma((n_chips,)), dma((n_chips,)),
            dma((n_chips,)), dma((n_chips,)), dma((n_chips,)), dma((n_chips,)),
            dma((n_chips,)), dma((n_chips,)),
            dma((n_chips,)), dma((n_chips,)), dma((2 * n_dp,)), dma((2 * n_dp,)),
        ],
        compiler_params=pltpu.CompilerParams(
            collective_id=0, has_side_effects=True, vmem_limit_bytes=63_400_000
        ),
        name="attention_router",
    )(
        starts, log_decay[0].T, norm_gain.reshape(heads, hd), router_new.T, router_old.T,
        queries[0], keys[0], values[0],
    )
    return logits.T[None], div[0, 0]


def solution(mesh):
    in_specs = (
        P("dp", "ctx", None),
        P("dp", "ctx", None),
        P("dp", "ctx", None),
        P("dp", "ctx", None),
        P("dp", None),
        P(),
        P(),
        P(),
    )
    out_specs = (P("dp", "ctx", None), P())
    return jax.shard_map(local, mesh=mesh, in_specs=in_specs, out_specs=out_specs, check_vma=False)
```

```python
import functools

import jax
import jax.numpy as jnp
from jax import lax
from jax.experimental import pallas as pl
from jax.experimental.pallas import tpu as pltpu
from jax.sharding import PartitionSpec as P

MESH = pl.DeviceIdType.MESH
F32 = jnp.float32
BF16 = jnp.bfloat16
NEG = -1e30
GROUP = 2
JOIN_LAG = 4
Z_CHIPS = 8


def split_two(x):
    hi = x.astype(BF16)
    return hi, (x - hi.astype(F32)).astype(BF16)


def body(
    n_dp, n_chips, n_z, n_tokens,
    starts_hbm, lam_hbm, gain_hbm, rnew_hbm, rold_hbm, q_hbm, k_hbm, v_hbm,
    logits_ref, div_ref,
    starts_ref, lam_ref, gain_ref, q_buf, k_buf, v_buf, rn_buf, ro_buf, intra_buf,
    c_buf, ct_buf, tail_buf, carried_buf, mask_buf,
    a_own, a_sib, w_own, w_recv, a_chip, a_all,
    s_own, s_send, s_recv, fwd_send, fwd_recv, ret_send, ret_recv,
    p_send, p_buf, acc_buf, red_mine, red_plane, red_part, red_all,
    load_sem, a_sems, ach_ssem, ach_rsem, s_ssem, s_rsem, fwd_ssem, fwd_rsem,
    ret_ssem, ret_rsem, p_ssem, p_rsem, plane_ssem, plane_rsem, all_ssem, all_rsem,
):
    tok, width = q_hbm.shape
    hd = gain_ref.shape[1]
    heads = gain_ref.shape[0]
    n_y = n_chips // n_z
    dp = lax.axis_index("dp")
    me = lax.axis_index("ctx")
    chip = lax.div(me, 2)
    core = lax.rem(me, 2)
    my_y = lax.div(chip, n_z)
    my_z = lax.rem(chip, n_z)
    sib = 2 * chip + (1 - core)

    def chip_at(i, sign):
        dy = lax.div(i, n_z)
        dz = lax.rem(i, n_z)
        if sign < 0:
            dy, dz = n_y - dy, n_z - dz
        return lax.rem(my_y + dy, n_y) * n_z + lax.rem(my_z + dz, n_z)

    def remote(src, dst, ssem, rsem, dp_to, ctx_to):
        return pltpu.make_async_remote_copy(
            src_ref=src, dst_ref=dst, send_sem=ssem, recv_sem=rsem,
            device_id=(dp_to, ctx_to), device_id_type=MESH,
        )

    part = width // n_y

    def load_part(j):
        cols = pl.ds(pl.multiple_of(lax.rem(my_y + j, n_y) * part, part), part)
        return (
            pltpu.make_async_copy(k_hbm.at[:, cols], k_buf.at[:, cols], load_sem.at[2 * j]),
            pltpu.make_async_copy(v_hbm.at[:, cols], v_buf.at[:, cols], load_sem.at[2 * j + 1]),
        )

    for copy in load_part(0):
        copy.start()
    small = (
        pltpu.make_async_copy(starts_hbm, starts_ref, load_sem.at[2 * n_y + 3]),
        pltpu.make_async_copy(lam_hbm, lam_ref, load_sem.at[2 * n_y + 4]),
        pltpu.make_async_copy(gain_hbm, gain_ref, load_sem.at[2 * n_y + 5]),
    )
    for copy in small:
        copy.start()

    barrier = pltpu.get_barrier_semaphore()
    rows_of = [lax.rem(my_y + dy, n_y) * n_z for dy in range(n_y)]
    places = [lax.rem(my_z + dz, n_z) for dz in range(n_z)]
    for dy in range(n_y):
        for dz in range(n_z):
            if dy or dz:
                to = 2 * (rows_of[dy] + places[dz]) + core
                pl.semaphore_signal(barrier, inc=1, device_id=(dp, to), device_id_type=MESH)
    me8 = 2 * dp + core
    n_all = 2 * n_dp

    def all_peer(i):
        to_core = core if i % 2 == 0 else 1 - core
        return lax.rem(dp + i // 2, n_dp), 2 * chip + to_core

    for i in range(1, n_all):
        pl.semaphore_signal(barrier, inc=1, device_id=all_peer(i), device_id_type=MESH)

    late = (
        pltpu.make_async_copy(q_hbm, q_buf, load_sem.at[2 * n_y]),
        pltpu.make_async_copy(rnew_hbm, rn_buf, load_sem.at[2 * n_y + 1]),
        pltpu.make_async_copy(rold_hbm, ro_buf, load_sem.at[2 * n_y + 2]),
    )

    for copy in small:
        copy.wait()

    base = me * tok
    n_seg = starts_ref.shape[1]

    def segment(pos):
        seg = (starts_ref[0, 0] <= pos).astype(jnp.int32)
        for j in range(1, n_seg):
            seg = seg + (starts_ref[0, j] <= pos).astype(jnp.int32)
        return seg

    seg_col = segment(base + lax.broadcasted_iota(jnp.int32, (tok, 1), 0))
    seg_row = segment(base + lax.broadcasted_iota(jnp.int32, (1, tok), 1))
    seg_before = segment(base - 1 + lax.broadcasted_iota(jnp.int32, (1, 1), 1))
    seg_end = segment(base + tok - 1 + lax.broadcasted_iota(jnp.int32, (1, 1), 1))
    later = lax.broadcasted_iota(jnp.int32, (tok, tok), 0)
    earlier = lax.broadcasted_iota(jnp.int32, (tok, tok), 1)
    mask_buf[...] = jnp.where((later >= earlier) & (seg_col == seg_row), 0.0, NEG)
    until = (later <= earlier).astype(BF16)
    ct = jnp.dot(lam_ref[...], until, preferred_element_type=F32)
    ct_buf[...] = ct
    c = jnp.concatenate([ct, jnp.zeros((128 - heads, tok), F32)], axis=0).T
    c_buf[...] = c
    carried_buf[...] = jnp.exp(c) * (seg_col == seg_before).astype(F32)
    total_c = ct[:, tok - 1 : tok]
    tail_buf[...] = jnp.exp(total_c - ct) * (seg_row == seg_end).astype(F32)
    decay = jnp.exp(total_c) * (seg_end == seg_before).astype(F32)
    a_own[...] = jnp.broadcast_to(decay, (heads, 128))

    def state_of(h):
        cols = pl.ds(pl.multiple_of(h * hd, hd), hd)
        kt = k_buf[:, cols].astype(F32).T * tail_buf[pl.ds(h, 1), :]
        hi, lo = split_two(kt)
        vh = v_buf[:, cols]
        return jnp.dot(hi, vh, preferred_element_type=F32) + jnp.dot(lo, vh, preferred_element_type=F32)

    def add_states(i):
        for j in range(n_y):
            @pl.when(i == j * n_z)
            def _():
                for copy in load_part(j):
                    copy.wait()
                if j + 1 < n_y:
                    for copy in load_part(j + 1):
                        copy.start()
                else:
                    for copy in late:
                        copy.start()

        slot = chip_at(i, 1)
        s_send[slot] = state_of(2 * slot + 1 - core).astype(BF16)
        s_own[slot] = state_of(2 * slot + core)

    def s_copy(slot):
        return remote(s_send.at[slot], s_recv.at[slot], s_ssem.at[slot], s_rsem.at[slot], dp, sib)

    def fwd_copy(slot):
        return remote(
            fwd_send.at[slot], fwd_recv.at[chip], fwd_ssem.at[slot], fwd_rsem.at[chip], dp, 2 * slot + core
        )

    def ach_copy(slot):
        to = 2 * slot + core
        return remote(a_chip.at[to], a_all.at[chip], ach_ssem.at[slot], ach_rsem.at[chip], dp, to)

    def join(i):
        slot = chip_at(i, 1)
        h = 2 * slot + core
        s_copy(slot).wait_recv()
        joined = w_own[pl.ds(h, 1), :] * s_own[slot] + w_recv[pl.ds(h, 1), :] * s_recv[slot].astype(F32)

        @pl.when(i > 0)
        def _():
            fwd_send[slot] = joined.astype(BF16)
            fwd_copy(slot).start()
            ach_copy(slot).start()

        @pl.when(i == 0)
        def _():
            fwd_recv[slot] = joined.astype(BF16)
            a_all[slot] = a_chip[h]

    add_states(0)
    pl.semaphore_wait(barrier, n_chips - 1 + n_all - 1)
    a_copy = remote(a_own, a_sib, a_sems.at[0], a_sems.at[1], dp, sib)
    a_copy.start()
    s_copy(chip).start()

    def first_states(i, carry):
        add_states(i)
        s_copy(chip_at(i, 1)).start()
        return carry

    lax.fori_loop(1, JOIN_LAG, first_states, 0)
    a_copy.wait()
    own, other = a_own[...], a_sib[...]
    w_own[...] = jnp.where(core == 0, other, 1.0)
    w_recv[...] = jnp.where(core == 0, 1.0, own)
    both_decay = own * other
    for h in range(heads):
        a_chip[h] = both_decay[h : h + 1, :]

    def phase_one(i, carry):
        @pl.when(i < n_chips)
        def _():
            add_states(i)
            s_copy(chip_at(i, 1)).start()

        join(i - JOIN_LAG)
        return carry

    lax.fori_loop(JOIN_LAG, n_chips + JOIN_LAG, phase_one, 0)

    late[0].wait()

    def phase_two(i, carry):
        for half in range(2):
            h = 2 * i + half
            cols = pl.ds(pl.multiple_of(h * hd, hd), hd)
            scores = lax.dot_general(
                q_buf[:, cols], k_buf[:, cols], (((1,), (1,)), ((), ())), preferred_element_type=F32
            )
            c_col = pltpu.roll(c_buf[...], lax.rem(128 - h, 128), 1)[:, 0:1]
            weight = jnp.exp(c_col - ct_buf[pl.ds(h, 1), :] + mask_buf[...])
            probs = (scores * weight).astype(BF16)
            intra_buf[:, cols] = jnp.dot(probs, v_buf[:, cols], preferred_element_type=F32)
        return carry

    lax.fori_loop(0, n_chips, phase_two, 0)

    def wait_states(i, carry):
        src = chip_at(i, -1)
        to = 2 * src + core
        remote(fwd_send.at[src], fwd_recv.at[src], fwd_ssem.at[src], fwd_rsem.at[src], dp, to).wait_recv()
        remote(a_chip.at[to], a_all.at[src], ach_ssem.at[src], ach_rsem.at[src], dp, to).wait_recv()
        return carry

    lax.fori_loop(1, n_chips, wait_states, 0)

    def scan_four(i, state):
        for j in range(4):
            src = 4 * i + j
            ret_send[src] = state.astype(BF16)
            state = a_all[src] * state + fwd_recv[src].astype(F32)
        return state

    lax.fori_loop(0, n_chips // 4, scan_four, jnp.zeros((hd, hd), F32))

    def ret_copy(slot):
        return remote(
            ret_send.at[slot], ret_recv.at[chip], ret_ssem.at[slot], ret_rsem.at[chip], dp, 2 * slot + core
        )

    def send_back(i, carry):
        ret_copy(chip_at(n_chips - i, 1)).start()
        return carry

    lax.fori_loop(1, n_chips, send_back, 0)
    ret_recv[chip] = ret_send[chip]
    late[1].wait()
    late[2].wait()
    acc_buf[...] = jnp.zeros_like(acc_buf)

    def p_copy(slot):
        return remote(p_send.at[slot], p_buf.at[slot, core], p_ssem.at[slot], p_rsem.at[slot], dp, sib)

    def head_out(slot, half):
        h = 2 * slot + half
        cols = pl.ds(pl.multiple_of(h * hd, hd), hd)
        hi, lo = split_two(p_buf[slot, half])
        qh = q_buf[:, cols]
        inter = jnp.dot(qh, hi, preferred_element_type=F32) + jnp.dot(qh, lo, preferred_element_type=F32)
        carried = pltpu.roll(carried_buf[...], lax.rem(128 - h, 128), 1)[:, 0:1]
        total = intra_buf[:, cols] + carried * inter
        meansq = jnp.mean(total * total, axis=1, keepdims=True) + 1e-06
        return split_two(total * lax.rsqrt(meansq) * gain_ref[pl.ds(h, 1), :])

    def hand_over(i):
        slot = chip_at(lax.rem(n_chips - i, n_chips), -1)
        h = 2 * slot + core

        @pl.when(i > 0)
        def _():
            remote(
                ret_send.at[slot], ret_recv.at[slot], ret_ssem.at[slot], ret_rsem.at[slot], dp, 2 * slot + core
            ).wait_recv()

        first = ret_recv[slot].astype(F32)

        @pl.when(core == 0)
        def _():
            p_buf[slot, core] = first
            p_send[slot] = a_own[pl.ds(h, 1), :] * first + s_own[slot]

        @pl.when(core == 1)
        def _():
            p_send[slot] = first
            p_buf[slot, core] = a_sib[pl.ds(h, 1), :] * first + s_recv[slot].astype(F32)

        p_copy(slot).start()

    def phase_three(i, carry):
        @pl.when(i < n_chips // GROUP)
        def _():
            for j in range(GROUP):
                hand_over(i * GROUP + j)

        @pl.when(i > 0)
        def _():
            slots = [chip_at(lax.rem(n_chips - (i - 1) * GROUP - j, n_chips), -1) for j in range(GROUP)]
            for slot in slots:
                remote(
                    p_send.at[slot], p_buf.at[slot, 1 - core], p_ssem.at[slot], p_rsem.at[slot], dp, sib
                ).wait_recv()
            outs = [[head_out(slot, half) for half in range(2)] for slot in slots]
            acc = acc_buf[...]
            for slot, (first, second) in zip(slots, outs):
                cols = pl.ds(pl.multiple_of(slot * 2 * hd, 2 * hd), 2 * hd)
                weights = jnp.concatenate([rn_buf[:, cols], ro_buf[:, cols]], axis=0)
                for x, y in zip(first, second):
                    acc = acc + lax.dot_general(
                        jnp.concatenate([x, y], axis=1), weights, (((1,), (1,)), ((), ())),
                        preferred_element_type=F32,
                    )
            acc_buf[...] = acc

        return carry

    lax.fori_loop(0, n_chips // GROUP + 1, phase_three, 0)

    n_exp = logits_ref.shape[0]
    both_logits = acc_buf[...].T
    new = both_logits[0:n_exp, :]
    old = both_logits[n_exp:, :]
    logits_ref[...] = new
    lp_new = new - jnp.log(jnp.sum(jnp.exp(new), axis=0, keepdims=True))
    lp_old = old - jnp.log(jnp.sum(jnp.exp(old), axis=0, keepdims=True))
    term = jnp.sum(jnp.exp(lp_old) * (lp_old - lp_new), axis=0, keepdims=True)
    mine = jnp.broadcast_to(jnp.sum(term, axis=1, keepdims=True), (1, 128))
    red_mine[...] = mine

    def plane_copy(dy, dz):
        i = dy * n_z + dz
        return remote(
            red_mine, red_plane.at[chip], plane_ssem.at[i], plane_rsem.at[i], dp,
            2 * (rows_of[dy] + places[dz]) + core,
        )

    plane_copies = [plane_copy(dy, dz) for dy in range(n_y) for dz in range(n_z) if dy or dz]
    for copy in plane_copies:
        copy.start()
    red_plane[chip] = mine

    def sent(i, carry):
        slot = chip_at(i, 1)
        s_copy(slot).wait_send()
        p_copy(slot).wait_send()

        @pl.when(i > 0)
        def _():
            fwd_copy(slot).wait_send()
            ret_copy(slot).wait_send()
            ach_copy(slot).wait_send()

        return carry

    lax.fori_loop(0, n_chips, sent, 0)
    for copy in plane_copies:
        copy.wait_recv()
    plane = jnp.sum(red_plane[...], axis=0)
    red_part[...] = plane

    def all_copy(i):
        return remote(red_part, red_all.at[me8], all_ssem.at[i], all_rsem.at[i], *all_peer(i))

    all_copies = [all_copy(i) for i in range(1, n_all)]
    for copy in all_copies:
        copy.start()
    red_all[me8] = plane
    for copy in plane_copies:
        copy.wait_send()
    for copy in all_copies:
        copy.wait()
    div_ref[...] = jnp.sum(red_all[...], axis=0) / n_tokens


def local(queries, keys, values, log_decay, starts, norm_gain, router_new, router_old):
    _, tok, width = queries.shape
    heads = log_decay.shape[2]
    hd = width // heads
    n_ctx = lax.axis_size("ctx")
    n_dp = lax.axis_size("dp")
    n_chips = n_ctx // 2
    n_z = min(Z_CHIPS, n_chips)
    n_y = n_chips // n_z
    n_exp = router_new.shape[1]
    vmem = pltpu.VMEM
    dma = pltpu.SemaphoreType.DMA
    hbm_spec = pl.BlockSpec(memory_space=pltpu.HBM)
    vmem_spec = pl.BlockSpec(memory_space=pltpu.VMEM)
    logits, div = pl.pallas_call(
        functools.partial(body, n_dp, n_chips, n_z, tok * n_ctx * n_dp),
        out_shape=(
            jax.ShapeDtypeStruct((n_exp, tok), F32),
            jax.ShapeDtypeStruct((1, 128), F32),
        ),
        in_specs=[
            hbm_spec, hbm_spec, hbm_spec, hbm_spec, hbm_spec, hbm_spec, hbm_spec, hbm_spec,
        ],
        out_specs=(vmem_spec, vmem_spec),
        scratch_shapes=[
            pltpu.SMEM(starts.shape, starts.dtype), vmem((heads, tok), BF16), vmem((heads, hd), F32),
            vmem((tok, width), BF16), vmem((tok, width), BF16), vmem((tok, width), BF16),
            vmem((n_exp, width), BF16), vmem((n_exp, width), BF16), vmem((tok, width), F32),
            vmem((tok, 128), F32), vmem((heads, tok), F32), vmem((heads, tok), F32), vmem((tok, 128), F32),
            vmem((tok, tok), F32),
            vmem((heads, 128), F32), vmem((heads, 128), F32), vmem((heads, 128), F32), vmem((heads, 128), F32),
            vmem((2 * n_chips, 1, 128), F32), vmem((n_chips, 1, 128), F32),
            vmem((n_chips, hd, hd), F32), vmem((n_chips, hd, hd), BF16), vmem((n_chips, hd, hd), BF16),
            vmem((n_chips, hd, hd), BF16), vmem((n_chips, hd, hd), BF16),
            vmem((n_chips, hd, hd), BF16), vmem((n_chips, hd, hd), BF16),
            vmem((n_chips, hd, hd), F32), vmem((n_chips, 2, hd, hd), F32),
            vmem((tok, 2 * n_exp), F32),
            vmem((1, 128), F32), vmem((n_chips, 1, 128), F32), vmem((1, 128), F32),
            vmem((2 * n_dp, 1, 128), F32),
            dma((2 * n_y + 6,)), dma((2,)), dma((n_chips,)), dma((n_chips,)), dma((n_chips,)), dma((n_chips,)),
            dma((n_chips,)), dma((n_chips,)), dma((n_chips,)), dma((n_chips,)),
            dma((n_chips,)), dma((n_chips,)),
            dma((n_chips,)), dma((n_chips,)), dma((2 * n_dp,)), dma((2 * n_dp,)),
        ],
        compiler_params=pltpu.CompilerParams(
            collective_id=0, has_side_effects=True, vmem_limit_bytes=63_400_000
        ),
        name="attention_router",
    )(
        starts, log_decay[0].T, norm_gain.reshape(heads, hd), router_new.T, router_old.T,
        queries[0], keys[0], values[0],
    )
    return logits.T[None], div[0, 0]


def solution(mesh):
    in_specs = (
        P("dp", "ctx", None),
        P("dp", "ctx", None),
        P("dp", "ctx", None),
        P("dp", "ctx", None),
        P("dp", None),
        P(),
        P(),
        P(),
    )
    out_specs = (P("dp", "ctx", None), P())
    return jax.shard_map(local, mesh=mesh, in_specs=in_specs, out_specs=out_specs, check_vma=False)
```

```python
import functools

import jax
import jax.numpy as jnp
from jax import lax
from jax.experimental import pallas as pl
from jax.experimental.pallas import tpu as pltpu
from jax.sharding import PartitionSpec as P

MESH = pl.DeviceIdType.MESH
F32 = jnp.float32
BF16 = jnp.bfloat16
NEG = -1e30
GROUP = 2
JOIN_LAG = 4
Z_CHIPS = 8


def split_two(x):
    hi = x.astype(BF16)
    return hi, (x - hi.astype(F32)).astype(BF16)


def body(
    n_dp, n_chips, n_z, n_tokens,
    starts_hbm, lam_hbm, gain_hbm, rnew_hbm, rold_hbm, q_hbm, k_hbm, v_hbm,
    logits_ref, div_ref,
    starts_ref, lam_ref, gain_ref, q_buf, k_buf, v_buf, rn_buf, ro_buf, intra_buf,
    c_buf, ct_buf, tail_buf, carried_buf, mask_buf,
    a_own, a_sib, w_own, w_recv, a_chip, a_all,
    s_own, s_send, s_recv, fwd_send, fwd_recv, ret_send, ret_recv,
    p_send, p_buf, acc_buf, red_mine, red_plane, red_part, red_all,
    load_sem, a_sems, ach_ssem, ach_rsem, s_ssem, s_rsem, fwd_ssem, fwd_rsem,
    ret_ssem, ret_rsem, p_ssem, p_rsem, plane_ssem, plane_rsem, all_ssem, all_rsem,
):
    tok, width = q_hbm.shape
    hd = gain_ref.shape[1]
    heads = gain_ref.shape[0]
    n_y = n_chips // n_z
    dp = lax.axis_index("dp")
    me = lax.axis_index("ctx")
    chip = lax.div(me, 2)
    core = lax.rem(me, 2)
    my_y = lax.div(chip, n_z)
    my_z = lax.rem(chip, n_z)
    sib = 2 * chip + (1 - core)

    def chip_at(i, sign):
        dy = lax.div(i, n_z)
        dz = lax.rem(i, n_z)
        if sign < 0:
            dy, dz = n_y - dy, n_z - dz
        return lax.rem(my_y + dy, n_y) * n_z + lax.rem(my_z + dz, n_z)

    def remote(src, dst, ssem, rsem, dp_to, ctx_to):
        return pltpu.make_async_remote_copy(
            src_ref=src, dst_ref=dst, send_sem=ssem, recv_sem=rsem,
            device_id=(dp_to, ctx_to), device_id_type=MESH,
        )

    part = width // n_y

    def load_part(j):
        cols = pl.ds(pl.multiple_of(lax.rem(my_y + j, n_y) * part, part), part)
        return (
            pltpu.make_async_copy(k_hbm.at[:, cols], k_buf.at[:, cols], load_sem.at[2 * j]),
            pltpu.make_async_copy(v_hbm.at[:, cols], v_buf.at[:, cols], load_sem.at[2 * j + 1]),
        )

    for copy in load_part(0):
        copy.start()
    small = (
        pltpu.make_async_copy(starts_hbm, starts_ref, load_sem.at[2 * n_y + 3]),
        pltpu.make_async_copy(lam_hbm, lam_ref, load_sem.at[2 * n_y + 4]),
        pltpu.make_async_copy(gain_hbm, gain_ref, load_sem.at[2 * n_y + 5]),
    )
    for copy in small:
        copy.start()

    barrier = pltpu.get_barrier_semaphore()
    rows_of = [lax.rem(my_y + dy, n_y) * n_z for dy in range(n_y)]
    places = [lax.rem(my_z + dz, n_z) for dz in range(n_z)]
    far_first = sorted(
        [(dy, dz) for dy in range(n_y) for dz in range(n_z) if dy or dz],
        key=lambda at: -min(at[0], n_y - at[0]) - min(at[1], n_z - at[1]),
    )
    for dy, dz in far_first:
        to = 2 * (rows_of[dy] + places[dz]) + core
        pl.semaphore_signal(barrier, inc=1, device_id=(dp, to), device_id_type=MESH)
    me8 = 2 * dp + core
    n_all = 2 * n_dp

    def all_peer(i):
        to_core = core if i % 2 == 0 else 1 - core
        return lax.rem(dp + i // 2, n_dp), 2 * chip + to_core

    for i in range(1, n_all):
        pl.semaphore_signal(barrier, inc=1, device_id=all_peer(i), device_id_type=MESH)

    late = (
        pltpu.make_async_copy(q_hbm, q_buf, load_sem.at[2 * n_y]),
        pltpu.make_async_copy(rnew_hbm, rn_buf, load_sem.at[2 * n_y + 1]),
        pltpu.make_async_copy(rold_hbm, ro_buf, load_sem.at[2 * n_y + 2]),
    )

    for copy in small:
        copy.wait()

    base = me * tok
    n_seg = starts_ref.shape[1]

    def segment(pos):
        seg = (starts_ref[0, 0] <= pos).astype(jnp.int32)
        for j in range(1, n_seg):
            seg = seg + (starts_ref[0, j] <= pos).astype(jnp.int32)
        return seg

    seg_col = segment(base + lax.broadcasted_iota(jnp.int32, (tok, 1), 0))
    seg_row = segment(base + lax.broadcasted_iota(jnp.int32, (1, tok), 1))
    seg_before = segment(base - 1 + lax.broadcasted_iota(jnp.int32, (1, 1), 1))
    seg_end = segment(base + tok - 1 + lax.broadcasted_iota(jnp.int32, (1, 1), 1))
    later = lax.broadcasted_iota(jnp.int32, (tok, tok), 0)
    earlier = lax.broadcasted_iota(jnp.int32, (tok, tok), 1)
    mask_buf[...] = jnp.where((later >= earlier) & (seg_col == seg_row), 0.0, NEG)
    until = (later <= earlier).astype(BF16)
    ct = jnp.dot(lam_ref[...], until, preferred_element_type=F32)
    ct_buf[...] = ct
    c = jnp.concatenate([ct, jnp.zeros((128 - heads, tok), F32)], axis=0).T
    c_buf[...] = c
    carried_buf[...] = jnp.exp(c) * (seg_col == seg_before).astype(F32)
    total_c = ct[:, tok - 1 : tok]
    tail_buf[...] = jnp.exp(total_c - ct) * (seg_row == seg_end).astype(F32)
    decay = jnp.exp(total_c) * (seg_end == seg_before).astype(F32)
    a_own[...] = jnp.broadcast_to(decay, (heads, 128))

    def state_of(h):
        cols = pl.ds(pl.multiple_of(h * hd, hd), hd)
        kt = k_buf[:, cols].astype(F32).T * tail_buf[pl.ds(h, 1), :]
        hi, lo = split_two(kt)
        vh = v_buf[:, cols]
        return jnp.dot(hi, vh, preferred_element_type=F32) + jnp.dot(lo, vh, preferred_element_type=F32)

    def add_states(i):
        for j in range(n_y):
            @pl.when(i == j * n_z)
            def _():
                for copy in load_part(j):
                    copy.wait()
                if j + 1 < n_y:
                    for copy in load_part(j + 1):
                        copy.start()
                else:
                    for copy in late:
                        copy.start()

        slot = chip_at(i, 1)
        s_send[slot] = state_of(2 * slot + 1 - core).astype(BF16)
        s_own[slot] = state_of(2 * slot + core)

    def s_copy(slot):
        return remote(s_send.at[slot], s_recv.at[slot], s_ssem.at[slot], s_rsem.at[slot], dp, sib)

    def fwd_copy(slot):
        return remote(
            fwd_send.at[slot], fwd_recv.at[chip], fwd_ssem.at[slot], fwd_rsem.at[chip], dp, 2 * slot + core
        )

    def ach_copy(slot):
        to = 2 * slot + core
        return remote(a_chip.at[to], a_all.at[chip], ach_ssem.at[slot], ach_rsem.at[chip], dp, to)

    def join(i):
        slot = chip_at(i, 1)
        h = 2 * slot + core
        s_copy(slot).wait_recv()
        joined = w_own[pl.ds(h, 1), :] * s_own[slot] + w_recv[pl.ds(h, 1), :] * s_recv[slot].astype(F32)

        @pl.when(i > 0)
        def _():
            fwd_send[slot] = joined.astype(BF16)
            fwd_copy(slot).start()
            ach_copy(slot).start()

        @pl.when(i == 0)
        def _():
            fwd_recv[slot] = joined.astype(BF16)
            a_all[slot] = a_chip[h]

    add_states(0)
    pl.semaphore_wait(barrier, n_chips - 1 + n_all - 1)
    a_copy = remote(a_own, a_sib, a_sems.at[0], a_sems.at[1], dp, sib)
    a_copy.start()
    s_copy(chip).start()

    def first_states(i, carry):
        add_states(i)
        s_copy(chip_at(i, 1)).start()
        return carry

    lax.fori_loop(1, JOIN_LAG, first_states, 0)
    a_copy.wait()
    own, other = a_own[...], a_sib[...]
    w_own[...] = jnp.where(core == 0, other, 1.0)
    w_recv[...] = jnp.where(core == 0, 1.0, own)
    both_decay = own * other
    for h in range(heads):
        a_chip[h] = both_decay[h : h + 1, :]

    def phase_one(i, carry):
        @pl.when(i < n_chips)
        def _():
            add_states(i)
            s_copy(chip_at(i, 1)).start()

        join(i - JOIN_LAG)
        return carry

    lax.fori_loop(JOIN_LAG, n_chips + JOIN_LAG, phase_one, 0)

    late[0].wait()

    def phase_two(i, carry):
        for half in range(2):
            h = 2 * i + half
            cols = pl.ds(pl.multiple_of(h * hd, hd), hd)
            scores = lax.dot_general(
                q_buf[:, cols], k_buf[:, cols], (((1,), (1,)), ((), ())), preferred_element_type=F32
            )
            c_col = pltpu.roll(c_buf[...], lax.rem(128 - h, 128), 1)[:, 0:1]
            weight = jnp.exp(c_col - ct_buf[pl.ds(h, 1), :] + mask_buf[...])
            probs = (scores * weight).astype(BF16)
            intra_buf[:, cols] = jnp.dot(probs, v_buf[:, cols], preferred_element_type=F32)
        return carry

    lax.fori_loop(0, n_chips, phase_two, 0)

    def wait_states(i, carry):
        src = chip_at(i, -1)
        to = 2 * src + core
        remote(fwd_send.at[src], fwd_recv.at[src], fwd_ssem.at[src], fwd_rsem.at[src], dp, to).wait_recv()
        remote(a_chip.at[to], a_all.at[src], ach_ssem.at[src], ach_rsem.at[src], dp, to).wait_recv()
        return carry

    lax.fori_loop(1, n_chips, wait_states, 0)

    def scan_four(i, state):
        for j in range(4):
            src = 4 * i + j
            ret_send[src] = state.astype(BF16)
            state = a_all[src] * state + fwd_recv[src].astype(F32)
        return state

    lax.fori_loop(0, n_chips // 4, scan_four, jnp.zeros((hd, hd), F32))

    def ret_copy(slot):
        return remote(
            ret_send.at[slot], ret_recv.at[chip], ret_ssem.at[slot], ret_rsem.at[chip], dp, 2 * slot + core
        )

    def send_back(i, carry):
        ret_copy(chip_at(n_chips - i, 1)).start()
        return carry

    lax.fori_loop(1, n_chips, send_back, 0)
    ret_recv[chip] = ret_send[chip]
    late[1].wait()
    late[2].wait()
    acc_buf[...] = jnp.zeros_like(acc_buf)

    def p_copy(slot):
        return remote(p_send.at[slot], p_buf.at[slot, core], p_ssem.at[slot], p_rsem.at[slot], dp, sib)

    def head_out(slot, half):
        h = 2 * slot + half
        cols = pl.ds(pl.multiple_of(h * hd, hd), hd)
        hi, lo = split_two(p_buf[slot, half])
        qh = q_buf[:, cols]
        inter = jnp.dot(qh, hi, preferred_element_type=F32) + jnp.dot(qh, lo, preferred_element_type=F32)
        carried = pltpu.roll(carried_buf[...], lax.rem(128 - h, 128), 1)[:, 0:1]
        total = intra_buf[:, cols] + carried * inter
        meansq = jnp.mean(total * total, axis=1, keepdims=True) + 1e-06
        return split_two(total * lax.rsqrt(meansq) * gain_ref[pl.ds(h, 1), :])

    def hand_over(i):
        slot = chip_at(lax.rem(n_chips - i, n_chips), -1)
        h = 2 * slot + core

        @pl.when(i > 0)
        def _():
            remote(
                ret_send.at[slot], ret_recv.at[slot], ret_ssem.at[slot], ret_rsem.at[slot], dp, 2 * slot + core
            ).wait_recv()

        first = ret_recv[slot].astype(F32)

        @pl.when(core == 0)
        def _():
            p_buf[slot, core] = first
            p_send[slot] = a_own[pl.ds(h, 1), :] * first + s_own[slot]

        @pl.when(core == 1)
        def _():
            p_send[slot] = first
            p_buf[slot, core] = a_sib[pl.ds(h, 1), :] * first + s_recv[slot].astype(F32)

        p_copy(slot).start()

    def phase_three(i, carry):
        @pl.when(i < n_chips // GROUP)
        def _():
            for j in range(GROUP):
                hand_over(i * GROUP + j)

        @pl.when(i > 0)
        def _():
            slots = [chip_at(lax.rem(n_chips - (i - 1) * GROUP - j, n_chips), -1) for j in range(GROUP)]
            for slot in slots:
                remote(
                    p_send.at[slot], p_buf.at[slot, 1 - core], p_ssem.at[slot], p_rsem.at[slot], dp, sib
                ).wait_recv()
            outs = [[head_out(slot, half) for half in range(2)] for slot in slots]
            acc = acc_buf[...]
            for slot, (first, second) in zip(slots, outs):
                cols = pl.ds(pl.multiple_of(slot * 2 * hd, 2 * hd), 2 * hd)
                weights = jnp.concatenate([rn_buf[:, cols], ro_buf[:, cols]], axis=0)
                for x, y in zip(first, second):
                    acc = acc + lax.dot_general(
                        jnp.concatenate([x, y], axis=1), weights, (((1,), (1,)), ((), ())),
                        preferred_element_type=F32,
                    )
            acc_buf[...] = acc

        return carry

    lax.fori_loop(0, n_chips // GROUP + 1, phase_three, 0)

    n_exp = logits_ref.shape[0]
    both_logits = acc_buf[...].T
    new = both_logits[0:n_exp, :]
    old = both_logits[n_exp:, :]
    logits_ref[...] = new
    lp_new = new - jnp.log(jnp.sum(jnp.exp(new), axis=0, keepdims=True))
    lp_old = old - jnp.log(jnp.sum(jnp.exp(old), axis=0, keepdims=True))
    term = jnp.sum(jnp.exp(lp_old) * (lp_old - lp_new), axis=0, keepdims=True)
    mine = jnp.broadcast_to(jnp.sum(term, axis=1, keepdims=True), (1, 128))
    red_mine[...] = mine

    def plane_copy(dy, dz):
        i = dy * n_z + dz
        return remote(
            red_mine, red_plane.at[chip], plane_ssem.at[i], plane_rsem.at[i], dp,
            2 * (rows_of[dy] + places[dz]) + core,
        )

    plane_copies = [plane_copy(dy, dz) for dy, dz in far_first]
    for copy in plane_copies:
        copy.start()
    red_plane[chip] = mine

    def sent(i, carry):
        slot = chip_at(i, 1)
        s_copy(slot).wait_send()
        p_copy(slot).wait_send()

        @pl.when(i > 0)
        def _():
            fwd_copy(slot).wait_send()
            ret_copy(slot).wait_send()
            ach_copy(slot).wait_send()

        return carry

    lax.fori_loop(0, n_chips, sent, 0)
    for copy in plane_copies:
        copy.wait_recv()
    plane = jnp.sum(red_plane[...], axis=0)
    red_part[...] = plane

    def all_copy(i):
        return remote(red_part, red_all.at[me8], all_ssem.at[i], all_rsem.at[i], *all_peer(i))

    all_copies = [all_copy(i) for i in range(1, n_all)]
    for copy in all_copies:
        copy.start()
    red_all[me8] = plane
    for copy in plane_copies:
        copy.wait_send()
    for copy in all_copies:
        copy.wait()
    div_ref[...] = jnp.sum(red_all[...], axis=0) / n_tokens


def local(queries, keys, values, log_decay, starts, norm_gain, router_new, router_old):
    _, tok, width = queries.shape
    heads = log_decay.shape[2]
    hd = width // heads
    n_ctx = lax.axis_size("ctx")
    n_dp = lax.axis_size("dp")
    n_chips = n_ctx // 2
    n_z = min(Z_CHIPS, n_chips)
    n_y = n_chips // n_z
    n_exp = router_new.shape[1]
    vmem = pltpu.VMEM
    dma = pltpu.SemaphoreType.DMA
    hbm_spec = pl.BlockSpec(memory_space=pltpu.HBM)
    vmem_spec = pl.BlockSpec(memory_space=pltpu.VMEM)
    logits, div = pl.pallas_call(
        functools.partial(body, n_dp, n_chips, n_z, tok * n_ctx * n_dp),
        out_shape=(
            jax.ShapeDtypeStruct((n_exp, tok), F32),
            jax.ShapeDtypeStruct((1, 128), F32),
        ),
        in_specs=[
            hbm_spec, hbm_spec, hbm_spec, hbm_spec, hbm_spec, hbm_spec, hbm_spec, hbm_spec,
        ],
        out_specs=(vmem_spec, vmem_spec),
        scratch_shapes=[
            pltpu.SMEM(starts.shape, starts.dtype), vmem((heads, tok), BF16), vmem((heads, hd), F32),
            vmem((tok, width), BF16), vmem((tok, width), BF16), vmem((tok, width), BF16),
            vmem((n_exp, width), BF16), vmem((n_exp, width), BF16), vmem((tok, width), F32),
            vmem((tok, 128), F32), vmem((heads, tok), F32), vmem((heads, tok), F32), vmem((tok, 128), F32),
            vmem((tok, tok), F32),
            vmem((heads, 128), F32), vmem((heads, 128), F32), vmem((heads, 128), F32), vmem((heads, 128), F32),
            vmem((2 * n_chips, 1, 128), F32), vmem((n_chips, 1, 128), F32),
            vmem((n_chips, hd, hd), F32), vmem((n_chips, hd, hd), BF16), vmem((n_chips, hd, hd), BF16),
            vmem((n_chips, hd, hd), BF16), vmem((n_chips, hd, hd), BF16),
            vmem((n_chips, hd, hd), BF16), vmem((n_chips, hd, hd), BF16),
            vmem((n_chips, hd, hd), F32), vmem((n_chips, 2, hd, hd), F32),
            vmem((tok, 2 * n_exp), F32),
            vmem((1, 128), F32), vmem((n_chips, 1, 128), F32), vmem((1, 128), F32),
            vmem((2 * n_dp, 1, 128), F32),
            dma((2 * n_y + 6,)), dma((2,)), dma((n_chips,)), dma((n_chips,)), dma((n_chips,)), dma((n_chips,)),
            dma((n_chips,)), dma((n_chips,)), dma((n_chips,)), dma((n_chips,)),
            dma((n_chips,)), dma((n_chips,)),
            dma((n_chips,)), dma((n_chips,)), dma((2 * n_dp,)), dma((2 * n_dp,)),
        ],
        compiler_params=pltpu.CompilerParams(
            collective_id=0, has_side_effects=True, vmem_limit_bytes=63_400_000
        ),
        name="attention_router",
    )(
        starts, log_decay[0].T, norm_gain.reshape(heads, hd), router_new.T, router_old.T,
        queries[0], keys[0], values[0],
    )
    return logits.T[None], div[0, 0]


def solution(mesh):
    in_specs = (
        P("dp", "ctx", None),
        P("dp", "ctx", None),
        P("dp", "ctx", None),
        P("dp", "ctx", None),
        P("dp", None),
        P(),
        P(),
        P(),
    )
    out_specs = (P("dp", "ctx", None), P())
    return jax.shard_map(local, mesh=mesh, in_specs=in_specs, out_specs=out_specs, check_vma=False)
```
